32 devices in a mesh: loop: 2 (over x), rep: 4 (over z), feat: 4 (over y, core).
Axes of the slice: x: 2, y: 2, z: 4, core: 2. Of those that a mesh axis runs over, the one named last changes fastest.
Arguments:
- features: bfloat16 [128, 2048], P('feat', 'loop'), may hold values from -6 to 6
- tile_values: bfloat16 [2, 4, 112, 128, 128], P('loop', 'rep'), may hold values from -0.1875 to 0.1875
- tile_coords: int32 [2, 4, 2, 112], P('loop', 'rep'), may hold values from 0 to 7, as said below
- section_counts: int32 [2, 4, 1], P('loop', 'rep'), may hold values from 0 to 64, as said below
- weight_one: bfloat16 [128, 128], replicated, may hold values from -0.5 to 0.5
- weight_two: bfloat16 [128, 128], replicated, may hold values from -0.5 to 0.5
- cotangent: bfloat16 [128, 2048], P(None, ('loop', 'feat')), may hold values from -24 to 24
Outputs:
- grad_one: float32 [128, 128], replicated
- grad_two: float32 [128, 128], replicated
- input_grad: bfloat16 [128, 2048], P('feat', 'loop')
The draws below stay inside these ranges and needn't reach their ends.
Inputs may be any that keep to these rules, and one draw needn't show every extreme that they name: `tile_coords`: slots of a list are grouped by section in order of sections; the live slots of one section name distinct (row, column) pairs; slots past the list's total count hold 0. `section_counts`: section k of rep index r covers the column block r + 4 * k places below the list's own loop index; sections with r + 4 * k of 2 or more hold 0.
All inputs are finite; a program needn't handle non-finite values.
Results may differ from the reference program's by a relative error of at most 0.029.
Values may be sent and summed in bfloat16 or wider, within the bound.
No kernel may reach another device: no remote copies, remote signals or barrier semaphores. Data moves between devices by JAX's collectives and lax.ppermute only.
A program may use at most 64 MiB of HBM per device.

```python
import math
import jax
import jax.numpy as jnp
from jax import lax

D = 128
TILE = 128
PANELS = 8
LOOPS = 2
REPLICAS = 4
SECTIONS = 1
TILE_DEV = 112
NODES = 2048


def tile_plan(key):
    base_key = jax.random.fold_in(key, 7)
    rep_ids = jnp.arange(REPLICAS, dtype=jnp.int32)[None, :, None]
    section_ids = jnp.arange(SECTIONS, dtype=jnp.int32)[None, None, :]
    offset = rep_ids + REPLICAS * section_ids
    distance = jnp.minimum(offset, LOOPS - offset)
    ceiling = jnp.minimum(40 // jnp.maximum(distance, 1), PANELS * PANELS)
    drawn = jax.random.randint(jax.random.fold_in(base_key, 1), (LOOPS, REPLICAS, SECTIONS), 0, ceiling + 1)
    counts = jnp.where(distance == 0, PANELS * PANELS, drawn)
    counts = jnp.where(offset >= LOOPS, 0, counts).astype(jnp.int32)
    pair_count = PANELS * PANELS
    scores = jax.random.randint(jax.random.fold_in(base_key, 2), (LOOPS, REPLICAS, SECTIONS, pair_count), 0, 2 ** 20)
    scores = scores * pair_count + jnp.arange(pair_count, dtype=jnp.int32)
    orders = jnp.argsort(scores, axis=-1).astype(jnp.int32)
    ends = jnp.cumsum(counts, axis=-1)
    starts = ends - counts
    slot_ids = jnp.arange(TILE_DEV, dtype=jnp.int32)
    section_of = jnp.sum((slot_ids[None, None, :, None] >= ends[:, :, None, :]).astype(jnp.int32), axis=-1)
    section_of = jnp.minimum(section_of, SECTIONS - 1)
    begin = jnp.take_along_axis(starts, section_of, axis=2)
    within = jnp.clip(slot_ids[None, None, :] - begin, 0, pair_count - 1)
    alive = slot_ids[None, None, :] < ends[:, :, -1:]
    flat_orders = orders.reshape(LOOPS, REPLICAS, SECTIONS * pair_count)
    pairs = jnp.take_along_axis(flat_orders, section_of * pair_count + within, axis=2)
    pairs = jnp.where(alive, pairs, 0)
    coords = jnp.stack([pairs // PANELS, pairs % PANELS], axis=2).astype(jnp.int32)
    return (counts, coords)


def draw_tile_coords(key, part):
    return tile_plan(key)[1]


def draw_section_counts(key, part):
    return tile_plan(key)[0]


def draw_cotangent(key, part):
    position = jnp.arange(NODES, dtype=jnp.float32) / max(NODES - 1, 1)
    rising = 1.0 + 2.0 * position
    value = jax.random.normal(key, (D, NODES), jnp.float32) * rising[None, :]
    return jnp.clip(value, -24.0, 24.0).astype(jnp.bfloat16)


def levels(stream_key, extent, cuts, smallest, high):
    factor_of = 1.0
    for dim, parts in cuts:
        heights = jax.random.uniform(jax.random.fold_in(jax.random.fold_in(stream_key, 6), dim), (parts,), jnp.float32, smallest / len(cuts), high / len(cuts))
        factor_of = factor_of * jnp.repeat(jnp.exp(heights), extent[dim] // parts).reshape((-1,) + (1,) * (len(extent) - 1 - dim))
    return factor_of


def scatter_about(own_key, dims, spread, reach, shards=(), kind=jnp.bfloat16):
    entries = spread * jax.random.normal(own_key, dims, jnp.float32)
    if shards:
        entries = entries * levels(own_key, dims, shards, -0.22, 0.18)
    return jnp.clip(entries, -reach, reach).astype(kind)


def setup_inputs(seed: int = 0) -> dict:
    seeds = jax.random.split(jax.random.key(seed), 8)
    return {
        "features": scatter_about(seeds[0], (D, NODES), 1.0, 6.0, ((0, 4), (1, 2))),
        "tile_values": scatter_about(seeds[1], (LOOPS, REPLICAS, TILE_DEV, TILE, TILE), (PANELS * TILE) ** -0.5, 0.1875, ((0, 2), (1, 4))),
        "tile_coords": draw_tile_coords(jax.random.fold_in(seeds[7], 71), 0),
        "section_counts": draw_section_counts(jax.random.fold_in(seeds[7], 71), 0),
        "weight_one": scatter_about(seeds[4], (D, D), D ** -0.5, 0.5),
        "weight_two": scatter_about(seeds[5], (D, D), D ** -0.5, 0.5),
        "cotangent": draw_cotangent(jax.random.fold_in(seeds[7], 71), 0),
    }


def slot_plan(tile_coords, section_counts):
    ends = jnp.cumsum(section_counts, axis=-1)
    slot_ids = jnp.arange(TILE_DEV, dtype=jnp.int32)
    section_ids = lax.optimization_barrier(jnp.sum((slot_ids[None, None, :, None] >= ends[:, :, None, :]).astype(jnp.int32), axis=-1))
    alive = slot_ids[None, None, :] < ends[:, :, -1:]
    section_ids = jnp.minimum(section_ids, SECTIONS - 1)
    loop_ids = jnp.arange(LOOPS, dtype=jnp.int32)[:, None, None]
    rep_ids = jnp.arange(REPLICAS, dtype=jnp.int32)[None, :, None]
    block_ids = jnp.mod(loop_ids - rep_ids - REPLICAS * section_ids, LOOPS)
    row_panels = tile_coords[:, :, 0, :]
    col_panels = block_ids * PANELS + tile_coords[:, :, 1, :]
    return (row_panels, col_panels, alive)

def apply_forward(source, tile_values, row_panels, col_panels, alive):
    width = source.shape[0]
    pieces = source.reshape(width, LOOPS * PANELS, TILE).transpose(1, 0, 2)
    panel_ids = jnp.arange(PANELS, dtype=jnp.int32)

    def one_loop(index):
        tiles_here = tile_values[index].reshape(-1, TILE, TILE).astype(jnp.float32)
        cols_here = col_panels[index].reshape(-1)
        rows_here = row_panels[index].reshape(-1)
        alive_here = alive[index].reshape(-1)
        picked = pieces[cols_here].astype(jnp.float32)
        products = jnp.einsum('bdc,bac->bda', picked, tiles_here, precision=lax.Precision.HIGHEST)
        placing = ((rows_here[:, None] == panel_ids[None, :]) & alive_here[:, None]).astype(jnp.float32)
        return jnp.einsum('bda,bp->dpa', products, placing, precision=lax.Precision.HIGHEST)
    blocks = lax.map(one_loop, jnp.arange(LOOPS, dtype=jnp.int32))
    return blocks.transpose(1, 0, 2, 3).reshape(width, NODES)

def apply_transposed(source, tile_values, row_panels, col_panels, alive):
    width = source.shape[0]
    pieces = source.reshape(width, LOOPS * PANELS, TILE).transpose(1, 0, 2)

    def one_loop(index, running):
        tiles_here = tile_values[index].reshape(-1, TILE, TILE).astype(jnp.float32)
        cols_here = col_panels[index].reshape(-1)
        rows_here = index * PANELS + row_panels[index].reshape(-1)
        alive_here = alive[index].reshape(-1).astype(jnp.float32)
        picked = pieces[rows_here].astype(jnp.float32)
        products = jnp.einsum('bda,bac->bdc', picked, tiles_here, precision=lax.Precision.HIGHEST)
        products = products * alive_here[:, None, None]
        return running.at[cols_here].add(products)
    start_sum = jnp.zeros((LOOPS * PANELS, width, TILE), jnp.float32)
    running = lax.fori_loop(0, LOOPS, one_loop, start_sum)
    return running.transpose(1, 0, 2).reshape(width, NODES)

def silu_slope(value):
    sigmoid_value = jax.nn.sigmoid(value)
    return sigmoid_value * (1.0 + value * (1.0 - sigmoid_value))

def reference(features, tile_values, tile_coords, section_counts, weight_one, weight_two, cotangent):
    row_panels, col_panels, alive = slot_plan(tile_coords, section_counts)
    scale = 1.0 / math.sqrt(NODES)
    mix_one = apply_forward(features, tile_values, row_panels, col_panels, alive).astype(jnp.bfloat16)
    z_one = jnp.dot(weight_one.T, mix_one, preferred_element_type=jnp.float32)
    h_one = jax.nn.silu(z_one).astype(jnp.bfloat16)
    mix_two = apply_forward(h_one, tile_values, row_panels, col_panels, alive).astype(jnp.bfloat16)
    z_two = jnp.dot(weight_two.T, mix_two, preferred_element_type=jnp.float32)
    dz_two = (cotangent * silu_slope(z_two)).astype(jnp.bfloat16)
    grad_two = jnp.dot(mix_two, dz_two.T, preferred_element_type=jnp.float32) * scale
    dm_two = jnp.dot(weight_two, dz_two, preferred_element_type=jnp.float32).astype(jnp.bfloat16)
    dh_one = apply_transposed(dm_two, tile_values, row_panels, col_panels, alive).astype(jnp.bfloat16)
    dz_one = (dh_one * silu_slope(z_one)).astype(jnp.bfloat16)
    grad_one = jnp.dot(mix_one, dz_one.T, preferred_element_type=jnp.float32) * scale
    dm_one = jnp.dot(weight_one, dz_one, preferred_element_type=jnp.float32).astype(jnp.bfloat16)
    input_grad = apply_transposed(dm_one, tile_values, row_panels, col_panels, alive).astype(jnp.bfloat16)
    return (grad_one, grad_two, input_grad)
```

```python
import functools
import math

import jax
import jax.numpy as jnp
from jax import lax
from jax.experimental import pallas as pl
from jax.experimental.pallas import tpu as pltpu
from jax.sharding import PartitionSpec as P

tile_batch = 8


def shortened(shard):

    def short(part):
        return part.astype(jnp.bfloat16) if part.dtype == jnp.float32 else part

    return jax.tree.map(short, shard)


def passed_along(value, axis, steps):
    count = lax.axis_size(axis)
    pairs = [(source, (source + steps) % count) for source in range(count)]
    return lax.ppermute(value, axis, pairs)


def silu_slope(argument):
    sigmoid_value = jax.nn.sigmoid(argument)
    return sigmoid_value * (1.0 + argument * (1.0 - sigmoid_value))


def section_term(source, section_id, layout, transposed, enabled=True):
    tile_set, row_ids, col_ids, starts, filled, panels = layout
    feat_width = source.shape[0]
    tile_side = tile_set.shape[-1]
    slot_total = tile_set.shape[0]
    shaped = source.reshape(feat_width, panels, tile_side)
    first = starts[section_id]
    number = jnp.where(enabled, filled[section_id], 0)
    rounds = (number + tile_batch - 1) // tile_batch
    offsets = jnp.arange(tile_batch, dtype=jnp.int32)
    panel_ids = jnp.arange(panels, dtype=jnp.int32)

    def one_round(round_id, running):
        within = round_id * tile_batch + offsets
        alive_mask = within < number
        slot_ids = jnp.minimum(first + within, slot_total - 1)
        chosen = tile_set[slot_ids]
        if transposed:
            picked = shaped[:, row_ids[slot_ids], :]
            products = jnp.einsum(
                "dba,bac->dbc", picked, chosen, preferred_element_type=jnp.float32
            )
            target = col_ids[slot_ids]
        else:
            picked = shaped[:, col_ids[slot_ids], :]
            products = jnp.einsum(
                "dbc,bac->dba", picked, chosen, preferred_element_type=jnp.float32
            )
            target = row_ids[slot_ids]
        placing = ((target[:, None] == panel_ids[None, :]) & alive_mask[:, None]).astype(
            jnp.float32
        )
        return running + jnp.einsum(
            "dbe,bp->dpe", products, placing, precision=lax.Precision.HIGHEST
        )

    zero_block = jnp.zeros((feat_width, panels, tile_side), jnp.float32)
    return lax.fori_loop(0, rounds, one_round, zero_block).reshape(feat_width, panels * tile_side)


def advance(block, stride):
    return jax.tree.map(
        lambda part, own: part.astype(own.dtype),
        passed_along(shortened(block), "loop", stride),
        block,
    )


def forward_product(source, layout):
    loop_size = lax.axis_size("loop")
    rep_size = lax.axis_size("rep")
    rep_index = lax.axis_index("rep")
    sections = -(-loop_size // rep_size)
    stride = rep_size % loop_size
    current = source
    for bit in range(rep_size.bit_length() - 1):
        jump = (1 << bit) % loop_size
        if jump:
            moved = passed_along(current, "loop", jump)
            current = jnp.where((rep_index >> bit) % 2 == 1, moved, current)
    running = section_term(current, 0, layout, False)
    if sections > 1:

        def onward(step_id, carry):
            ahead, acc = carry
            ahead = advance(ahead, stride)
            return (ahead, acc + section_term(ahead, step_id, layout, False))

        ahead, running = lax.fori_loop(1, sections, onward, (current, running))
    return running


def transposed_product(source, layout):
    loop_size = lax.axis_size("loop")
    rep_size = lax.axis_size("rep")
    rep_index = lax.axis_index("rep")
    sections = -(-loop_size // rep_size)
    stride = rep_size % loop_size
    running = section_term(source, sections - 1, layout, True)
    if sections > 1:

        def backward(step_id, acc):
            acc = jax.tree.map(
                lambda part, own: part.astype(own.dtype),
                passed_along(shortened(acc), "loop", -stride),
                acc,
            )
            return acc + section_term(source, sections - 1 - step_id, layout, True)

        running = lax.fori_loop(1, sections, backward, running)
    for bit in range(rep_size.bit_length() - 1):
        jump = (1 << bit) % loop_size
        if jump:
            moved = passed_along(running.astype(jnp.bfloat16), "loop", -jump).astype(running.dtype)
            running = jnp.where((rep_index >> bit) % 2 == 1, moved, running)
    return running


def to_nodes(partial_value):
    summed = lax.psum(partial_value.astype(jnp.bfloat16), "rep")
    return lax.all_to_all(summed, "feat", split_axis=1, concat_axis=0, tiled=True)


def to_features(node_block):
    return lax.all_to_all(node_block, "feat", split_axis=0, concat_axis=1, tiled=True)


def weight_grad(mixed, slope):
    part_sum = jnp.einsum("dq,eq->de", mixed, slope, preferred_element_type=jnp.float32)
    return lax.psum(part_sum, ("loop", "feat"))


def ring_shards(features, tile_values, tile_coords, section_counts, weight_one, weight_two, cotangent):
    tile_set = tile_values[0, 0]
    row_ids = tile_coords[0, 0, 0]
    col_ids = tile_coords[0, 0, 1]
    filled = section_counts[0, 0]
    starts = jnp.cumsum(filled) - filled
    panels = features.shape[1] // tile_set.shape[-1]
    layout = (tile_set, row_ids, col_ids, starts, filled, panels)
    scale = 1.0 / math.sqrt(features.shape[1] * lax.axis_size("loop"))
    mix_one = to_nodes(forward_product(features, layout))
    z_one = jnp.einsum("de,dq->eq", weight_one, mix_one, preferred_element_type=jnp.float32)
    h_one = jax.nn.silu(z_one).astype(jnp.bfloat16)
    mix_two = to_nodes(forward_product(to_features(h_one), layout))
    z_two = jnp.einsum("de,dq->eq", weight_two, mix_two, preferred_element_type=jnp.float32)
    dz_two = (cotangent * silu_slope(z_two)).astype(jnp.bfloat16)
    grad_two = weight_grad(mix_two, dz_two) * scale
    dm_two = jnp.einsum("de,eq->dq", weight_two, dz_two, preferred_element_type=jnp.float32).astype(
        jnp.bfloat16
    )
    dh_one = to_nodes(transposed_product(to_features(dm_two), layout))
    dz_one = (dh_one * silu_slope(z_one)).astype(jnp.bfloat16)
    grad_one = weight_grad(mix_one, dz_one) * scale
    dm_one = jnp.einsum("de,eq->dq", weight_one, dz_one, preferred_element_type=jnp.float32).astype(
        jnp.bfloat16
    )
    partial_value = transposed_product(to_features(dm_one), layout)
    input_grad = lax.psum(partial_value.astype(jnp.bfloat16), "rep")
    return (grad_one, grad_two, input_grad)


mesh_axes = ("loop", "rep", "feat")
vmem_bytes = 24 * 1024 * 1024


def routed(value, target):
    loops, reps, feats = (lax.axis_size(axis) for axis in mesh_axes)
    pairs = []
    for i in range(loops):
        for r in range(reps):
            for f in range(feats):
                to_loop, to_rep, to_feat = target(i, r, f)
                pairs.append(
                    ((i * reps + r) * feats + f, (to_loop * reps + to_rep) * feats + to_feat)
                )
    return lax.ppermute(value, mesh_axes, pairs)


def to_other_core(i, r, f):
    return i, r, f ^ 1


def to_other_pair(i, r, f):
    return i, r, f ^ 2


def to_other_loop(i, r, f):
    return 1 - i, r, f


def to_other_rep(i, r, f):
    return i, r ^ 1, f


def to_far_rep(i, r, f):
    return i, r ^ 2, f


def to_row_owner(i, r, f):
    return (i, r - 1, f) if r % 2 else (1 - i, r + 1, f)


def to_column_owner(i, r, f):
    return (1 - i, r - 1, f) if r % 2 else (i, r + 1, f)


def to_feature_pair(i, r, f):
    return (1 - i if r % 2 else i), r, f ^ 2


def local_call(kernel, outs, operands, spaces=None, scratch=(), flops=0):
    spaces = spaces or [pltpu.VMEM] * len(operands)
    moved = sum(o.size * o.dtype.itemsize for o in operands) + sum(
        math.prod(o.shape) * 4 for o in outs
    )
    return pl.pallas_call(
        kernel,
        out_shape=list(outs),
        in_specs=[pl.BlockSpec(memory_space=space) for space in spaces],
        out_specs=[pl.BlockSpec(memory_space=pltpu.VMEM) for _ in outs],
        scratch_shapes=list(scratch),
        compiler_params=pltpu.CompilerParams(vmem_limit_bytes=vmem_bytes),
        cost_estimate=pl.CostEstimate(flops=flops, bytes_accessed=moved, transcendentals=0),
    )(*operands)


def bf16_array(*shape):
    return jax.ShapeDtypeStruct(shape, jnp.bfloat16)


def f32_array(*shape):
    return jax.ShapeDtypeStruct(shape, jnp.float32)


def dot_nn(a, b):
    return lax.dot_general(a, b, (((1,), (0,)), ((), ())), preferred_element_type=jnp.float32)


def dot_nt(a, b):
    return lax.dot_general(a, b, (((1,), (1,)), ((), ())), preferred_element_type=jnp.float32)


def dot_tn(a, b):
    return lax.dot_general(a, b, (((0,), (0,)), ((), ())), preferred_element_type=jnp.float32)


def place_kernel(panels, side, ids_ref, count_ref, coords_ref, tiles_ref, block_ref, sems):
    block_ref[...] = jnp.zeros_like(block_ref)
    quarter = panels // 4
    core = ids_ref[2] % 2
    count = count_ref[0]

    def position(panel):
        part = panel // quarter
        half = jnp.bitwise_xor(part % 2, core)
        return (half * 2 + part // 2) * quarter + panel % quarter

    def tile_copy(slot):
        row = pl.multiple_of(position(coords_ref[0, slot]) * side, side)
        col = pl.multiple_of(position(coords_ref[1, slot]) * side, side)
        return pltpu.make_async_copy(
            tiles_ref.at[slot],
            block_ref.at[pl.ds(row, side), pl.ds(col, side)],
            sems.at[slot],
        )

    def begin(slot, carry):
        tile_copy(slot).start()
        return carry

    def finish(slot, carry):
        tile_copy(slot).wait()
        return carry

    lax.fori_loop(0, count, begin, 0)
    lax.fori_loop(0, count, finish, 0)


def first_kernel(ids_ref, own_ref, across_ref, pair_ref, swapped_ref, block_ref, out_ref, full):
    width, nodes = own_ref.shape
    odd = ids_ref[1] % 2 == 1
    feat = ids_ref[2]
    core = feat % 2
    quarter = nodes // 4
    half = nodes // 2

    def keep(value, owner):
        row = pl.multiple_of(owner * width, width)
        for part in range(4):
            lane = pl.multiple_of(
                jnp.bitwise_xor(part % 2, core) * half + (part // 2) * quarter, quarter
            )
            full[pl.ds(row, width), pl.ds(lane, quarter)] = value[
                :, part * quarter : (part + 1) * quarter
            ]

    keep(jnp.where(odd, across_ref[...], own_ref[...]), feat)
    keep(pair_ref[...], jnp.bitwise_xor(feat, 2))
    keep(swapped_ref[:width, :], jnp.bitwise_xor(feat, 1))
    keep(swapped_ref[width:, :], jnp.bitwise_xor(feat, 3))
    out_ref[...] = dot_nt(full[...], block_ref[:half, :]).astype(out_ref.dtype)


def forward_kernel(own_ref, other_ref, block_ref, out_ref):
    half = own_ref.shape[1]
    total = dot_nt(own_ref[...], block_ref[:half, :half])
    total += dot_nt(other_ref[...], block_ref[:half, half:])
    out_ref[...] = total.astype(out_ref.dtype)


def backward_kernel(own_ref, other_ref, block_ref, out_ref):
    half = own_ref.shape[1]
    width = out_ref.shape[1]
    total = dot_nn(own_ref[...], block_ref[:half, :width])
    total += dot_nn(other_ref[...], block_ref[half:, :width])
    out_ref[...] = total.astype(out_ref.dtype)


def summed(ids_ref, own_ref, near_ref, across_ref):
    odd = ids_ref[1] % 2 == 1
    second = jnp.where(odd, across_ref[...], own_ref[...])
    return (near_ref[...].astype(jnp.float32) + second.astype(jnp.float32)).astype(jnp.bfloat16)


def slope(value):
    part = jax.nn.sigmoid(value)
    return part * (1.0 + value * (1.0 - part))


def layer_one_kernel(ids_ref, own_ref, near_ref, across_ref, weight_ref, mix_ref, h_ref):
    mix = summed(ids_ref, own_ref, near_ref, across_ref)
    mix_ref[...] = mix
    z = dot_tn(weight_ref[...], mix)
    h_ref[...] = (z * jax.nn.sigmoid(z)).astype(h_ref.dtype)


def layer_two_kernel(
    ids_ref, own_ref, near_ref, weight_ref, cot_ref, cot_pair_ref, mix_ref, dz_ref, dm_ref
):
    mix = (own_ref[...].astype(jnp.float32) + near_ref[...].astype(jnp.float32)).astype(
        jnp.bfloat16
    )
    mix_ref[...] = mix
    z = dot_tn(weight_ref[...], mix)
    upper = ids_ref[2] // 2 == 1
    mine, pair = cot_ref[...], cot_pair_ref[...]
    quarter = mine.shape[1]
    rate = slope(z)
    low = (jnp.where(upper, pair, mine).astype(jnp.float32) * rate[:, :quarter]).astype(
        jnp.bfloat16
    )
    high = (jnp.where(upper, mine, pair).astype(jnp.float32) * rate[:, quarter:]).astype(
        jnp.bfloat16
    )
    dz_ref[:, :quarter] = low
    dz_ref[:, quarter:] = high
    dm_ref[...] = dot_nn(weight_ref[...], dz_ref[...]).astype(dm_ref.dtype)


def slope_kernel(ids_ref, mix_ref, across_ref, weight_ref, own_mix_ref, slope_ref):
    odd = ids_ref[1] % 2 == 1
    mix = jnp.where(odd, across_ref[...], mix_ref[...])
    own_mix_ref[...] = mix
    slope_ref[...] = slope(dot_tn(weight_ref[...], mix))


def back_one_kernel(
    ids_ref, own_ref, near_ref, across_ref, slope_ref, weight_ref, dz_ref, dm_ref, send_ref
):
    dh = summed(ids_ref, own_ref, near_ref, across_ref)
    dz = (dh.astype(jnp.float32) * slope_ref[...]).astype(jnp.bfloat16)
    dz_ref[...] = dz
    width = dm_ref.shape[0]
    feat = ids_ref[2]
    mine = pl.multiple_of(feat * width, width)
    theirs = pl.multiple_of(jnp.bitwise_xor(feat, 1) * width, width)
    dm_ref[...] = dot_nn(weight_ref[pl.ds(mine, width), :], dz).astype(dm_ref.dtype)
    send_ref[...] = dot_nn(weight_ref[pl.ds(theirs, width), :], dz).astype(send_ref.dtype)


def grad_kernel(mix_ref, slope_ref, out_ref):
    out_ref[...] = dot_nt(mix_ref[...], slope_ref[...])


def sum_kernel(ids_ref, own_ref, near_ref, across_ref, out_ref):
    out_ref[...] = summed(ids_ref, own_ref, near_ref, across_ref)


def last_kernel(ids_ref, own_ref, far_ref, out_ref):
    core = ids_ref[2] % 2
    nodes = own_ref.shape[1]
    quarter = nodes // 4
    half = nodes // 2
    for part in range(4):
        lane = pl.multiple_of(
            jnp.bitwise_xor(part % 2, core) * half + (part // 2) * quarter, quarter
        )
        here = pl.ds(lane, quarter)
        out_ref[:, part * quarter : (part + 1) * quarter] = own_ref[:, here] + far_ref[:, here]


def grad_total(part, scale):
    part = part + routed(part, to_other_core)
    part = part + routed(part, to_other_loop)
    return (part + routed(part, to_far_rep)) * scale


def paired_shards(
    features, tile_values, tile_coords, section_counts, weight_one, weight_two, cotangent
):
    hidden = weight_one.shape[0]
    width, nodes = features.shape
    side = tile_values.shape[-1]
    panels = nodes // side
    half = nodes // 2
    scale = 1.0 / math.sqrt(nodes * lax.axis_size("loop"))
    ids = jnp.stack([lax.axis_index(axis) for axis in mesh_axes]).astype(jnp.int32)
    smem, vmem = pltpu.SMEM, pltpu.VMEM

    across = routed(features, to_other_loop)
    pair = routed(features, to_feature_pair)
    cot_pair = routed(cotangent, to_other_pair)
    (block,) = local_call(
        functools.partial(place_kernel, panels, side),
        [bf16_array(nodes, nodes)],
        [ids, section_counts[0, 0], tile_coords[0, 0], tile_values[0, 0]],
        [smem, smem, smem, pl.ANY],
        [pltpu.SemaphoreType.DMA((panels * panels,))],
        flops=4_000_000_000,
    )
    odd = lax.axis_index("rep") % 2 == 1
    swapped = routed(
        jnp.concatenate([jnp.where(odd, across, features), pair], axis=0), to_other_core
    )
    product_flops = 2 * hidden * nodes * half

    (part_one,) = local_call(
        first_kernel,
        [bf16_array(hidden, half)],
        [ids, features, across, pair, swapped, block],
        [smem] + [vmem] * 5,
        [pltpu.VMEM((hidden, nodes), jnp.bfloat16)],
        flops=product_flops,
    )
    mix_one, h_one = local_call(
        layer_one_kernel,
        [bf16_array(hidden, half)] * 2,
        [ids, part_one, routed(part_one, to_row_owner), routed(part_one, to_other_loop), weight_one],
        [smem] + [vmem] * 4,
    )
    (part_two,) = local_call(
        forward_kernel,
        [bf16_array(hidden, half)],
        [h_one, routed(h_one, to_other_core), block],
        flops=product_flops,
    )
    mix_two, dz_two, dm_two = local_call(
        layer_two_kernel,
        [bf16_array(hidden, half)] * 3,
        [ids, part_two, routed(part_two, to_other_rep), weight_two, cotangent, cot_pair],
        [smem] + [vmem] * 5,
    )
    mix_here, slope_here = local_call(
        slope_kernel,
        [bf16_array(hidden, half), f32_array(hidden, half)],
        [ids, mix_one, routed(mix_one, to_other_loop), weight_one],
        [smem] + [vmem] * 3,
    )
    (part_three,) = local_call(
        backward_kernel,
        [bf16_array(hidden, half)],
        [dm_two, routed(dm_two, to_other_core), block],
        flops=product_flops,
    )
    (grad_two,) = local_call(grad_kernel, [f32_array(hidden, hidden)], [mix_two, dz_two])
    grad_two = grad_total(grad_two, scale)
    dz_one, dm_one, dm_send = local_call(
        back_one_kernel,
        [bf16_array(hidden, half), bf16_array(width, half), bf16_array(width, half)],
        [
            ids,
            part_three,
            routed(part_three, to_column_owner),
            routed(part_three, to_other_loop),
            slope_here,
            weight_one,
        ],
        [smem] + [vmem] * 5,
    )
    (part_four,) = local_call(
        backward_kernel,
        [bf16_array(width, nodes)],
        [dm_one, routed(dm_send, to_other_core), block],
        flops=product_flops,
    )
    (grad_one,) = local_call(grad_kernel, [f32_array(hidden, hidden)], [mix_here, dz_one])
    grad_one = grad_total(grad_one, scale)
    (near_sum,) = local_call(
        sum_kernel,
        [bf16_array(width, nodes)],
        [ids, part_four, routed(part_four, to_column_owner), routed(part_four, to_other_loop)],
        [smem] + [vmem] * 3,
    )
    (input_grad,) = local_call(
        last_kernel,
        [bf16_array(width, nodes)],
        [ids, near_sum, routed(near_sum, to_far_rep)],
        [smem] + [vmem] * 2,
    )
    return (grad_one, grad_two, input_grad)


def solution(mesh):
    sizes = dict(mesh.shape)
    paired = sizes["loop"] == 2 and sizes["rep"] == 4 and sizes["feat"] == 4
    return jax.shard_map(
        paired_shards if paired else ring_shards,
        mesh=mesh,
        in_specs=(
            P("feat", "loop"),
            P("loop", "rep", None, None, None),
            P("loop", "rep", None, None),
            P("loop", "rep", None),
            P(),
            P(),
            P(None, ("loop", "feat")),
        ),
        out_specs=(P(), P(), P("feat", "loop")),
        check_vma=False,
    )
```

```python
import functools
import math

import jax
import jax.numpy as jnp
from jax import lax
from jax.experimental import pallas as pl
from jax.experimental.pallas import tpu as pltpu
from jax.sharding import PartitionSpec as P

tile_batch = 8


def shortened(shard):

    def short(part):
        return part.astype(jnp.bfloat16) if part.dtype == jnp.float32 else part

    return jax.tree.map(short, shard)


def passed_along(value, axis, steps):
    count = lax.axis_size(axis)
    pairs = [(source, (source + steps) % count) for source in range(count)]
    return lax.ppermute(value, axis, pairs)


def silu_slope(argument):
    sigmoid_value = jax.nn.sigmoid(argument)
    return sigmoid_value * (1.0 + argument * (1.0 - sigmoid_value))


def section_term(source, section_id, layout, transposed, enabled=True):
    tile_set, row_ids, col_ids, starts, filled, panels = layout
    feat_width = source.shape[0]
    tile_side = tile_set.shape[-1]
    slot_total = tile_set.shape[0]
    shaped = source.reshape(feat_width, panels, tile_side)
    first = starts[section_id]
    number = jnp.where(enabled, filled[section_id], 0)
    rounds = (number + tile_batch - 1) // tile_batch
    offsets = jnp.arange(tile_batch, dtype=jnp.int32)
    panel_ids = jnp.arange(panels, dtype=jnp.int32)

    def one_round(round_id, running):
        within = round_id * tile_batch + offsets
        alive_mask = within < number
        slot_ids = jnp.minimum(first + within, slot_total - 1)
        chosen = tile_set[slot_ids]
        if transposed:
            picked = shaped[:, row_ids[slot_ids], :]
            products = jnp.einsum(
                "dba,bac->dbc", picked, chosen, preferred_element_type=jnp.float32
            )
            target = col_ids[slot_ids]
        else:
            picked = shaped[:, col_ids[slot_ids], :]
            products = jnp.einsum(
                "dbc,bac->dba", picked, chosen, preferred_element_type=jnp.float32
            )
            target = row_ids[slot_ids]
        placing = ((target[:, None] == panel_ids[None, :]) & alive_mask[:, None]).astype(
            jnp.float32
        )
        return running + jnp.einsum(
            "dbe,bp->dpe", products, placing, precision=lax.Precision.HIGHEST
        )

    zero_block = jnp.zeros((feat_width, panels, tile_side), jnp.float32)
    return lax.fori_loop(0, rounds, one_round, zero_block).reshape(feat_width, panels * tile_side)


def advance(block, stride):
    return jax.tree.map(
        lambda part, own: part.astype(own.dtype),
        passed_along(shortened(block), "loop", stride),
        block,
    )


def forward_product(source, layout):
    loop_size = lax.axis_size("loop")
    rep_size = lax.axis_size("rep")
    rep_index = lax.axis_index("rep")
    sections = -(-loop_size // rep_size)
    stride = rep_size % loop_size
    current = source
    for bit in range(rep_size.bit_length() - 1):
        jump = (1 << bit) % loop_size
        if jump:
            moved = passed_along(current, "loop", jump)
            current = jnp.where((rep_index >> bit) % 2 == 1, moved, current)
    running = section_term(current, 0, layout, False)
    if sections > 1:

        def onward(step_id, carry):
            ahead, acc = carry
            ahead = advance(ahead, stride)
            return (ahead, acc + section_term(ahead, step_id, layout, False))

        ahead, running = lax.fori_loop(1, sections, onward, (current, running))
    return running


def transposed_product(source, layout):
    loop_size = lax.axis_size("loop")
    rep_size = lax.axis_size("rep")
    rep_index = lax.axis_index("rep")
    sections = -(-loop_size // rep_size)
    stride = rep_size % loop_size
    running = section_term(source, sections - 1, layout, True)
    if sections > 1:

        def backward(step_id, acc):
            acc = jax.tree.map(
                lambda part, own: part.astype(own.dtype),
                passed_along(shortened(acc), "loop", -stride),
                acc,
            )
            return acc + section_term(source, sections - 1 - step_id, layout, True)

        running = lax.fori_loop(1, sections, backward, running)
    for bit in range(rep_size.bit_length() - 1):
        jump = (1 << bit) % loop_size
        if jump:
            moved = passed_along(running.astype(jnp.bfloat16), "loop", -jump).astype(running.dtype)
            running = jnp.where((rep_index >> bit) % 2 == 1, moved, running)
    return running


def to_nodes(partial_value):
    summed = lax.psum(partial_value.astype(jnp.bfloat16), "rep")
    return lax.all_to_all(summed, "feat", split_axis=1, concat_axis=0, tiled=True)


def to_features(node_block):
    return lax.all_to_all(node_block, "feat", split_axis=0, concat_axis=1, tiled=True)


def weight_grad(mixed, slope):
    part_sum = jnp.einsum("dq,eq->de", mixed, slope, preferred_element_type=jnp.float32)
    return lax.psum(part_sum, ("loop", "feat"))


def ring_shards(features, tile_values, tile_coords, section_counts, weight_one, weight_two, cotangent):
    tile_set = tile_values[0, 0]
    row_ids = tile_coords[0, 0, 0]
    col_ids = tile_coords[0, 0, 1]
    filled = section_counts[0, 0]
    starts = jnp.cumsum(filled) - filled
    panels = features.shape[1] // tile_set.shape[-1]
    layout = (tile_set, row_ids, col_ids, starts, filled, panels)
    scale = 1.0 / math.sqrt(features.shape[1] * lax.axis_size("loop"))
    mix_one = to_nodes(forward_product(features, layout))
    z_one = jnp.einsum("de,dq->eq", weight_one, mix_one, preferred_element_type=jnp.float32)
    h_one = jax.nn.silu(z_one).astype(jnp.bfloat16)
    mix_two = to_nodes(forward_product(to_features(h_one), layout))
    z_two = jnp.einsum("de,dq->eq", weight_two, mix_two, preferred_element_type=jnp.float32)
    dz_two = (cotangent * silu_slope(z_two)).astype(jnp.bfloat16)
    grad_two = weight_grad(mix_two, dz_two) * scale
    dm_two = jnp.einsum("de,eq->dq", weight_two, dz_two, preferred_element_type=jnp.float32).astype(
        jnp.bfloat16
    )
    dh_one = to_nodes(transposed_product(to_features(dm_two), layout))
    dz_one = (dh_one * silu_slope(z_one)).astype(jnp.bfloat16)
    grad_one = weight_grad(mix_one, dz_one) * scale
    dm_one = jnp.einsum("de,eq->dq", weight_one, dz_one, preferred_element_type=jnp.float32).astype(
        jnp.bfloat16
    )
    partial_value = transposed_product(to_features(dm_one), layout)
    input_grad = lax.psum(partial_value.astype(jnp.bfloat16), "rep")
    return (grad_one, grad_two, input_grad)


mesh_axes = ("loop", "rep", "feat")
vmem_bytes = 24 * 1024 * 1024


def routed(value, target):
    loops, reps, feats = (lax.axis_size(axis) for axis in mesh_axes)
    pairs = []
    for i in range(loops):
        for r in range(reps):
            for f in range(feats):
                to_loop, to_rep, to_feat = target(i, r, f)
                pairs.append(
                    ((i * reps + r) * feats + f, (to_loop * reps + to_rep) * feats + to_feat)
                )
    return lax.ppermute(value, mesh_axes, pairs)


def to_other_core(i, r, f):
    return i, r, f ^ 1


def to_other_pair(i, r, f):
    return i, r, f ^ 2


def to_other_loop(i, r, f):
    return 1 - i, r, f


def to_other_rep(i, r, f):
    return i, r ^ 1, f


def to_row_owner(i, r, f):
    return (i, r - 1, f) if r % 2 else (1 - i, r + 1, f)


def to_column_owner(i, r, f):
    return (1 - i, r - 1, f) if r % 2 else (i, r + 1, f)


def to_far_column_owner(i, r, f):
    return (1 - i if r % 2 else i), r ^ 2, f


def to_last_column_owner(i, r, f):
    return (1 - i if r % 2 else i), r ^ 3, f


def to_feature_pair(i, r, f):
    return (1 - i if r % 2 else i), r, f ^ 2


def local_call(kernel, outs, operands, spaces=None, scratch=(), flops=0):
    spaces = spaces or [pltpu.VMEM] * len(operands)
    moved = sum(o.size * o.dtype.itemsize for o in operands) + sum(
        math.prod(o.shape) * 4 for o in outs
    )
    return pl.pallas_call(
        kernel,
        out_shape=list(outs),
        in_specs=[pl.BlockSpec(memory_space=space) for space in spaces],
        out_specs=[pl.BlockSpec(memory_space=pltpu.VMEM) for _ in outs],
        scratch_shapes=list(scratch),
        compiler_params=pltpu.CompilerParams(vmem_limit_bytes=vmem_bytes),
        cost_estimate=pl.CostEstimate(flops=flops, bytes_accessed=moved, transcendentals=0),
    )(*operands)


def bf16_array(*shape):
    return jax.ShapeDtypeStruct(shape, jnp.bfloat16)


def f32_array(*shape):
    return jax.ShapeDtypeStruct(shape, jnp.float32)


def dot_nn(a, b):
    return lax.dot_general(a, b, (((1,), (0,)), ((), ())), preferred_element_type=jnp.float32)


def dot_nt(a, b):
    return lax.dot_general(a, b, (((1,), (1,)), ((), ())), preferred_element_type=jnp.float32)


def place_kernel(
    panels,
    side,
    count_ref,
    coords_ref,
    tiles_ref,
    block_ref,
    coords,
    list_sem,
    sems,
):
    lists = pltpu.make_async_copy(coords_ref, coords, list_sem)
    lists.start()
    block_ref[...] = jnp.zeros_like(block_ref)
    quarter = panels // 4
    core = lax.axis_index("feat") % 2
    lists.wait()
    count = count_ref[0]

    def start_of(panel):
        part = panel // quarter
        half = jnp.bitwise_xor(part % 2, core)
        return pl.multiple_of(((half * 2 + part // 2) * quarter + panel % quarter) * side, side)

    def tile_copy(slot):
        return pltpu.make_async_copy(
            tiles_ref.at[0, 0, slot],
            block_ref.at[
                pl.ds(start_of(coords[0, 0, 0, slot]), side),
                pl.ds(start_of(coords[0, 0, 1, slot]), side),
            ],
            sems.at[slot],
        )

    def in_groups(act):
        group = 8

        def some(index, carry):
            for offset in range(group):
                act(index * group + offset)
            return carry

        def one(slot, carry):
            act(slot)
            return carry

        whole = count // group
        lax.fori_loop(0, whole, some, 0)
        lax.fori_loop(whole * group, count, one, 0)

    in_groups(lambda slot: tile_copy(slot).start())
    in_groups(lambda slot: tile_copy(slot).wait())


def turn_kernel(one_ref, two_ref, one_turned_ref, two_turned_ref):
    one_turned_ref[...] = one_ref[...].T
    two_turned_ref[...] = two_ref[...].T


def first_kernel(
    own_ref,
    across_ref,
    pair_ref,
    own_swap_ref,
    across_swap_ref,
    pair_swap_ref,
    block_ref,
    out_ref,
    full,
):
    width, nodes = own_ref.shape
    odd = lax.axis_index("rep") % 2 == 1
    feat = lax.axis_index("feat")
    core = feat % 2
    quarter = nodes // 4
    half = nodes // 2

    def keep(value, owner):
        row = pl.multiple_of(owner * width, width)
        for part in range(4):
            lane = pl.multiple_of(
                jnp.bitwise_xor(part % 2, core) * half + (part // 2) * quarter, quarter
            )
            full[pl.ds(row, width), pl.ds(lane, quarter)] = value[
                :, part * quarter : (part + 1) * quarter
            ]

    keep(jnp.where(odd, across_ref[...], own_ref[...]), feat)
    keep(jnp.where(odd, across_swap_ref[...], own_swap_ref[...]), jnp.bitwise_xor(feat, 1))
    keep(pair_ref[...], jnp.bitwise_xor(feat, 2))
    keep(pair_swap_ref[...], jnp.bitwise_xor(feat, 3))
    out_ref[...] = dot_nt(full[...], block_ref[:half, :]).astype(out_ref.dtype)


def forward_kernel(own_ref, other_ref, block_ref, out_ref):
    half = own_ref.shape[1]
    total = dot_nt(own_ref[...], block_ref[:half, :half])
    total += dot_nt(other_ref[...], block_ref[:half, half:])
    out_ref[...] = total.astype(out_ref.dtype)


def backward_kernel(own_ref, other_ref, block_ref, out_ref):
    half = own_ref.shape[1]
    total = dot_nn(own_ref[...], block_ref[:half, :half])
    total += dot_nn(other_ref[...], block_ref[half:, :half])
    out_ref[...] = total.astype(out_ref.dtype)


def summed(own_ref, near_ref, across_ref):
    odd = lax.axis_index("rep") % 2 == 1
    second = jnp.where(odd, across_ref[...], own_ref[...])
    return (near_ref[...].astype(jnp.float32) + second.astype(jnp.float32)).astype(jnp.bfloat16)


def slope(value):
    part = jax.nn.sigmoid(value)
    return part * (1.0 + value * (1.0 - part))


def layer_one_kernel(own_ref, near_ref, across_ref, turned_ref, mix_ref, h_ref):
    mix = summed(own_ref, near_ref, across_ref)
    mix_ref[...] = mix
    z = dot_nn(turned_ref[...], mix)
    h_ref[...] = (z * jax.nn.sigmoid(z)).astype(h_ref.dtype)


def layer_two_kernel(
    own_ref,
    near_ref,
    turned_ref,
    weight_ref,
    cot_ref,
    cot_pair_ref,
    mix_ref,
    dz_ref,
    dm_ref,
):
    total = own_ref[...].astype(jnp.float32) + near_ref[...].astype(jnp.float32)
    mix = total.astype(jnp.bfloat16)
    mix_ref[...] = mix
    rate = slope(dot_nn(turned_ref[...], mix))
    upper = lax.axis_index("feat") // 2 == 1
    mine, pair = cot_ref[...], cot_pair_ref[...]
    quarter = mine.shape[1]
    low, high = jnp.where(upper, pair, mine), jnp.where(upper, mine, pair)
    dz_ref[:, :quarter] = (low.astype(jnp.float32) * rate[:, :quarter]).astype(jnp.bfloat16)
    dz_ref[:, quarter:] = (high.astype(jnp.float32) * rate[:, quarter:]).astype(jnp.bfloat16)
    dm_ref[...] = dot_nn(weight_ref[...], dz_ref[...]).astype(dm_ref.dtype)


def slope_kernel(mix_ref, across_ref, turned_ref, here_ref, slope_ref):
    odd = lax.axis_index("rep") % 2 == 1
    mix = jnp.where(odd, across_ref[...], mix_ref[...])
    here_ref[...] = mix
    slope_ref[...] = slope(dot_nn(turned_ref[...], mix))


def grad_kernel(mix_ref, slope_ref, out_ref):
    out_ref[...] = dot_nt(mix_ref[...], slope_ref[...])


def back_one_kernel(own_ref, near_ref, across_ref, slope_ref, dz_ref):
    dh = summed(own_ref, near_ref, across_ref)
    dz_ref[...] = (dh.astype(jnp.float32) * slope_ref[...]).astype(dz_ref.dtype)


def message_kernel(
    dz_ref,
    dz_swap_ref,
    weight_ref,
    block_ref,
    mix_ref,
    mix_swap_ref,
    two_ref,
    two_swap_ref,
    out_ref,
):
    feat = lax.axis_index("feat")
    width = out_ref.shape[0] // 2
    hidden = weight_ref.shape[0]
    half = dz_ref.shape[1]
    mix, mix_swap, dz, dz_swap = mix_ref[...], mix_swap_ref[...], dz_ref[...], dz_swap_ref[...]
    rows = weight_ref[pl.ds(pl.multiple_of(feat * width, width), width), :]
    own = dot_nn(rows, dz).astype(jnp.bfloat16)
    other = dot_nn(rows, dz_swap).astype(jnp.bfloat16)
    total = dot_nn(own, block_ref[:half, :]) + dot_nn(other, block_ref[half:, :])
    out_ref[:width, :] = total.astype(out_ref.dtype)
    swap = feat % 2 == 1
    one = dot_nt(jnp.where(swap, mix_swap, mix), jnp.where(swap, dz_swap, dz)) + dot_nt(
        jnp.where(swap, mix, mix_swap), jnp.where(swap, dz, dz_swap)
    )
    two = two_ref[...] + two_swap_ref[...]
    count = hidden // width
    for index, grad in enumerate((one, two)):
        grad = grad.astype(out_ref.dtype)
        for part in range(count):
            lane = (index * count + part) * hidden
            out_ref[width:, lane : lane + hidden] = grad[part * width : (part + 1) * width, :]


def last_kernel(
    scale,
    own_ref,
    near_ref,
    across_ref,
    far_ref,
    far_near_ref,
    one_ref,
    two_ref,
    out_ref,
):
    odd = lax.axis_index("rep") % 2 == 1
    core = lax.axis_index("feat") % 2
    width, nodes = out_ref.shape
    hidden = one_ref.shape[0]
    quarter = nodes // 4
    half = nodes // 2

    def total(rows, columns):
        refs = (near_ref, far_ref, far_near_ref)
        value = jnp.where(odd, across_ref[rows, columns], own_ref[rows, columns])
        value = value.astype(jnp.float32)
        for ref in refs:
            value += ref[rows, columns].astype(jnp.float32)
        return value

    for part in range(4):
        lane = pl.multiple_of(
            jnp.bitwise_xor(part % 2, core) * half + (part // 2) * quarter, quarter
        )
        out_ref[:, part * quarter : (part + 1) * quarter] = total(
            pl.ds(0, width), pl.ds(lane, quarter)
        ).astype(out_ref.dtype)
    count = hidden // width
    for index, grad_ref in enumerate((one_ref, two_ref)):
        for part in range(count):
            lane = (index * count + part) * hidden
            grad_ref[part * width : (part + 1) * width, :] = (
                total(pl.ds(width, width), pl.ds(lane, hidden)) * scale
            )


def paired_shards(
    features, tile_values, tile_coords, section_counts, weight_one, weight_two, cotangent
):
    hidden = weight_one.shape[0]
    width, nodes = features.shape
    side = tile_values.shape[-1]
    panels = nodes // side
    half = nodes // 2
    scale = 1.0 / math.sqrt(nodes * lax.axis_size("loop"))
    product_flops = 2 * hidden * nodes * half

    across = routed(features, to_other_loop)
    pair = routed(features, to_feature_pair)
    own_swap = routed(features, to_other_core)
    (block,) = local_call(
        functools.partial(place_kernel, panels, side),
        [bf16_array(nodes, nodes)],
        [section_counts[0, 0]]
        + [
            pltpu.with_memory_space_constraint(value, pltpu.HBM)
            for value in (tile_coords, tile_values)
        ],
        [pltpu.SMEM, pltpu.HBM, pltpu.HBM],
        [
            pltpu.SMEM(tile_coords.shape, jnp.int32),
            pltpu.SemaphoreType.DMA,
            pltpu.SemaphoreType.DMA((panels * panels,)),
        ],
        flops=4_000_000_000,
    )
    one_turned, two_turned = local_call(
        turn_kernel,
        [bf16_array(hidden, hidden)] * 2,
        [weight_one, lax.optimization_barrier((weight_two, block))[0]],
    )
    across, pair, block = lax.optimization_barrier((across, pair, block))
    (part_one,) = local_call(
        first_kernel,
        [bf16_array(hidden, half)],
        [
            features,
            across,
            pair,
            own_swap,
            routed(across, to_other_core),
            routed(pair, to_other_core),
            block,
        ],
        None,
        [pltpu.VMEM((hidden, nodes), jnp.bfloat16)],
        flops=product_flops,
    )
    cot_pair = routed(lax.optimization_barrier((cotangent, part_one))[0], to_other_pair)
    near_one = routed(part_one, to_row_owner)
    across_one = routed(part_one, to_other_loop)
    mix_one, h_one = local_call(
        layer_one_kernel,
        [bf16_array(hidden, half)] * 2,
        [part_one, near_one, across_one, one_turned],
        None,
    )
    (part_two,) = local_call(
        forward_kernel,
        [bf16_array(hidden, half)],
        [h_one, routed(h_one, to_other_core), block],
        flops=product_flops,
    )
    near_two, mix_across, cot_pair = lax.optimization_barrier(
        (routed(part_two, to_other_rep), routed(mix_one, to_other_loop), cot_pair)
    )
    mix_two, dz_two, dm_two = local_call(
        layer_two_kernel,
        [bf16_array(hidden, half)] * 3,
        [part_two, near_two, two_turned, weight_two, cotangent, cot_pair],
        None,
    )
    (part_three,) = local_call(
        backward_kernel,
        [bf16_array(hidden, half)],
        [dm_two, routed(dm_two, to_other_core), block],
        flops=product_flops,
    )
    (grad_two,) = local_call(grad_kernel, [f32_array(hidden, hidden)], [mix_two, dz_two])
    mix_here, slope_here = local_call(
        slope_kernel,
        [bf16_array(hidden, half), f32_array(hidden, half)],
        [mix_one, lax.optimization_barrier((mix_across, part_three))[0], one_turned],
        None,
    )
    (dz_one,) = local_call(
        back_one_kernel,
        [bf16_array(hidden, half)],
        [
            part_three,
            routed(part_three, to_column_owner),
            routed(part_three, to_other_loop),
            slope_here,
        ],
        None,
    )
    (message,) = local_call(
        message_kernel,
        [bf16_array(2 * width, nodes)],
        [
            dz_one,
            routed(dz_one, to_other_core),
            weight_one,
            block,
            mix_here,
            routed(mix_here, to_other_core),
            grad_two,
            routed(grad_two, to_other_core),
        ],
        None,
        flops=product_flops,
    )
    return tuple(
        local_call(
            functools.partial(last_kernel, scale),
            [f32_array(hidden, hidden), f32_array(hidden, hidden), bf16_array(width, nodes)],
            [
                    message,
                routed(message, to_column_owner),
                routed(message, to_other_loop),
                routed(message, to_far_column_owner),
                routed(message, to_last_column_owner),
            ],
            None,
        )
    )


def solution(mesh):
    sizes = dict(mesh.shape)
    paired = sizes["loop"] == 2 and sizes["rep"] == 4 and sizes["feat"] == 4
    return jax.shard_map(
        paired_shards if paired else ring_shards,
        mesh=mesh,
        in_specs=(
            P("feat", "loop"),
            P("loop", "rep", None, None, None),
            P("loop", "rep", None, None),
            P("loop", "rep", None),
            P(),
            P(),
            P(None, ("loop", "feat")),
        ),
        out_specs=(P(), P(), P("feat", "loop")),
        check_vma=False,
    )
```

```python
import functools
import math

import jax
import jax.numpy as jnp
from jax import lax
from jax.experimental import pallas as pl
from jax.experimental.pallas import tpu as pltpu
from jax.sharding import PartitionSpec as P

tile_batch = 8


def shortened(shard):

    def short(part):
        return part.astype(jnp.bfloat16) if part.dtype == jnp.float32 else part

    return jax.tree.map(short, shard)


def passed_along(value, axis, steps):
    count = lax.axis_size(axis)
    pairs = [(source, (source + steps) % count) for source in range(count)]
    return lax.ppermute(value, axis, pairs)


def silu_slope(argument):
    sigmoid_value = jax.nn.sigmoid(argument)
    return sigmoid_value * (1.0 + argument * (1.0 - sigmoid_value))


def section_term(source, section_id, layout, transposed, enabled=True):
    tile_set, row_ids, col_ids, starts, filled, panels = layout
    feat_width = source.shape[0]
    tile_side = tile_set.shape[-1]
    slot_total = tile_set.shape[0]
    shaped = source.reshape(feat_width, panels, tile_side)
    first = starts[section_id]
    number = jnp.where(enabled, filled[section_id], 0)
    rounds = (number + tile_batch - 1) // tile_batch
    offsets = jnp.arange(tile_batch, dtype=jnp.int32)
    panel_ids = jnp.arange(panels, dtype=jnp.int32)

    def one_round(round_id, running):
        within = round_id * tile_batch + offsets
        alive_mask = within < number
        slot_ids = jnp.minimum(first + within, slot_total - 1)
        chosen = tile_set[slot_ids]
        if transposed:
            picked = shaped[:, row_ids[slot_ids], :]
            products = jnp.einsum(
                "dba,bac->dbc", picked, chosen, preferred_element_type=jnp.float32
            )
            target = col_ids[slot_ids]
        else:
            picked = shaped[:, col_ids[slot_ids], :]
            products = jnp.einsum(
                "dbc,bac->dba", picked, chosen, preferred_element_type=jnp.float32
            )
            target = row_ids[slot_ids]
        placing = ((target[:, None] == panel_ids[None, :]) & alive_mask[:, None]).astype(
            jnp.float32
        )
        return running + jnp.einsum(
            "dbe,bp->dpe", products, placing, precision=lax.Precision.HIGHEST
        )

    zero_block = jnp.zeros((feat_width, panels, tile_side), jnp.float32)
    return lax.fori_loop(0, rounds, one_round, zero_block).reshape(feat_width, panels * tile_side)


def advance(block, stride):
    return jax.tree.map(
        lambda part, own: part.astype(own.dtype),
        passed_along(shortened(block), "loop", stride),
        block,
    )


def forward_product(source, layout):
    loop_size = lax.axis_size("loop")
    rep_size = lax.axis_size("rep")
    rep_index = lax.axis_index("rep")
    sections = -(-loop_size // rep_size)
    stride = rep_size % loop_size
    current = source
    for bit in range(rep_size.bit_length() - 1):
        jump = (1 << bit) % loop_size
        if jump:
            moved = passed_along(current, "loop", jump)
            current = jnp.where((rep_index >> bit) % 2 == 1, moved, current)
    running = section_term(current, 0, layout, False)
    if sections > 1:

        def onward(step_id, carry):
            ahead, acc = carry
            ahead = advance(ahead, stride)
            return (ahead, acc + section_term(ahead, step_id, layout, False))

        ahead, running = lax.fori_loop(1, sections, onward, (current, running))
    return running


def transposed_product(source, layout):
    loop_size = lax.axis_size("loop")
    rep_size = lax.axis_size("rep")
    rep_index = lax.axis_index("rep")
    sections = -(-loop_size // rep_size)
    stride = rep_size % loop_size
    running = section_term(source, sections - 1, layout, True)
    if sections > 1:

        def backward(step_id, acc):
            acc = jax.tree.map(
                lambda part, own: part.astype(own.dtype),
                passed_along(shortened(acc), "loop", -stride),
                acc,
            )
            return acc + section_term(source, sections - 1 - step_id, layout, True)

        running = lax.fori_loop(1, sections, backward, running)
    for bit in range(rep_size.bit_length() - 1):
        jump = (1 << bit) % loop_size
        if jump:
            moved = passed_along(running.astype(jnp.bfloat16), "loop", -jump).astype(running.dtype)
            running = jnp.where((rep_index >> bit) % 2 == 1, moved, running)
    return running


def to_nodes(partial_value):
    summed = lax.psum(partial_value.astype(jnp.bfloat16), "rep")
    return lax.all_to_all(summed, "feat", split_axis=1, concat_axis=0, tiled=True)


def to_features(node_block):
    return lax.all_to_all(node_block, "feat", split_axis=0, concat_axis=1, tiled=True)


def weight_grad(mixed, slope):
    part_sum = jnp.einsum("dq,eq->de", mixed, slope, preferred_element_type=jnp.float32)
    return lax.psum(part_sum, ("loop", "feat"))


def ring_shards(features, tile_values, tile_coords, section_counts, weight_one, weight_two, cotangent):
    tile_set = tile_values[0, 0]
    row_ids = tile_coords[0, 0, 0]
    col_ids = tile_coords[0, 0, 1]
    filled = section_counts[0, 0]
    starts = jnp.cumsum(filled) - filled
    panels = features.shape[1] // tile_set.shape[-1]
    layout = (tile_set, row_ids, col_ids, starts, filled, panels)
    scale = 1.0 / math.sqrt(features.shape[1] * lax.axis_size("loop"))
    mix_one = to_nodes(forward_product(features, layout))
    z_one = jnp.einsum("de,dq->eq", weight_one, mix_one, preferred_element_type=jnp.float32)
    h_one = jax.nn.silu(z_one).astype(jnp.bfloat16)
    mix_two = to_nodes(forward_product(to_features(h_one), layout))
    z_two = jnp.einsum("de,dq->eq", weight_two, mix_two, preferred_element_type=jnp.float32)
    dz_two = (cotangent * silu_slope(z_two)).astype(jnp.bfloat16)
    grad_two = weight_grad(mix_two, dz_two) * scale
    dm_two = jnp.einsum("de,eq->dq", weight_two, dz_two, preferred_element_type=jnp.float32).astype(
        jnp.bfloat16
    )
    dh_one = to_nodes(transposed_product(to_features(dm_two), layout))
    dz_one = (dh_one * silu_slope(z_one)).astype(jnp.bfloat16)
    grad_one = weight_grad(mix_one, dz_one) * scale
    dm_one = jnp.einsum("de,eq->dq", weight_one, dz_one, preferred_element_type=jnp.float32).astype(
        jnp.bfloat16
    )
    partial_value = transposed_product(to_features(dm_one), layout)
    input_grad = lax.psum(partial_value.astype(jnp.bfloat16), "rep")
    return (grad_one, grad_two, input_grad)


mesh_axes = ("loop", "rep", "feat")
vmem_bytes = 24 * 1024 * 1024


def routed(value, target, outward=False):
    loops, reps, feats = (lax.axis_size(axis) for axis in mesh_axes)
    pairs = []
    for i in range(loops):
        for r in range(reps):
            for f in range(feats):
                idle = r >= loops
                if idle and outward:
                    continue
                to_loop, to_rep, to_feat = to_other_core(i, r, f) if idle else target(i, r, f)
                pairs.append(
                    ((i * reps + r) * feats + f, (to_loop * reps + to_rep) * feats + to_feat)
                )
    return lax.ppermute(value, mesh_axes, pairs)


def to_other_core(i, r, f):
    return i, r, f ^ 1


def to_other_pair(i, r, f):
    return i, r, f ^ 2


def to_other_loop(i, r, f):
    return 1 - i, r, f


def to_odd_across(i, r, f):
    return (1 - i, r, f) if r % 2 else (i, r, f ^ 1)


def to_other_rep(i, r, f):
    return i, r ^ 1, f


def to_row_owner(i, r, f):
    return (i, r - 1, f) if r % 2 else (1 - i, r + 1, f)


def to_column_owner(i, r, f):
    return (1 - i, r - 1, f) if r % 2 else (i, r + 1, f)


def to_far_rep(i, r, f):
    return i, r ^ 2, f


def to_far_column_owner(i, r, f):
    return (1 - i if r % 2 else i), r ^ 2, f


def to_last_column_owner(i, r, f):
    return (1 - i if r % 2 else i), r ^ 3, f


def to_feature_pair(i, r, f):
    return (1 - i if r % 2 else i), r, f ^ 2


def local_call(kernel, outs, operands, spaces=None, scratch=(), flops=0):
    spaces = spaces or [pltpu.VMEM] * len(operands)
    moved = sum(o.size * o.dtype.itemsize for o in operands) + sum(
        math.prod(o.shape) * 4 for o in outs
    )
    return pl.pallas_call(
        kernel,
        out_shape=list(outs),
        in_specs=[pl.BlockSpec(memory_space=space) for space in spaces],
        out_specs=[pl.BlockSpec(memory_space=pltpu.VMEM) for _ in outs],
        scratch_shapes=list(scratch),
        compiler_params=pltpu.CompilerParams(vmem_limit_bytes=vmem_bytes),
        cost_estimate=pl.CostEstimate(flops=flops, bytes_accessed=moved, transcendentals=0),
    )(*operands)


def bf16_array(*shape):
    return jax.ShapeDtypeStruct(shape, jnp.bfloat16)


def f32_array(*shape):
    return jax.ShapeDtypeStruct(shape, jnp.float32)


def dot_nn(a, b):
    return lax.dot_general(a, b, (((1,), (0,)), ((), ())), preferred_element_type=jnp.float32)


def dot_nt(a, b):
    return lax.dot_general(a, b, (((1,), (1,)), ((), ())), preferred_element_type=jnp.float32)


def place_kernel(
    panels,
    side,
    count_ref,
    coords_ref,
    tiles_ref,
    block_ref,
    coords,
    held,
    list_sem,
    sems,
):
    chunks = sems.shape[0]
    size = held.shape[0] // chunks
    lists = pltpu.make_async_copy(coords_ref, coords, list_sem)
    lists.start()
    copies = []
    for chunk in range(chunks):
        here = pl.ds(chunk * size, size)
        copies.append(
            pltpu.make_async_copy(tiles_ref.at[0, 0, here], held.at[here], sems.at[chunk])
        )
        copies[-1].start()
    block_ref[...] = jnp.zeros_like(block_ref)
    quarter = panels // 4
    core = lax.axis_index("feat") % 2
    lists.wait()
    count = count_ref[0]

    def start_of(panel):
        part = panel // quarter
        half = jnp.bitwise_xor(part % 2, core)
        return pl.multiple_of(((half * 2 + part // 2) * quarter + panel % quarter) * side, side)

    def place(slot, carry):
        rows = pl.ds(start_of(coords[0, 0, 0, slot]), side)
        columns = pl.ds(start_of(coords[0, 0, 1, slot]), side)
        block_ref[rows, columns] = held[slot]
        return carry

    group = 4

    def place_group(index, carry):
        for offset in range(group):
            place(index * group + offset, carry)
        return carry

    for chunk in range(chunks):
        copies[chunk].wait()
        end = jnp.minimum(count, (chunk + 1) * size)
        whole = end // group
        lax.fori_loop(chunk * size // group, whole, place_group, 0)
        lax.fori_loop(jnp.maximum(whole * group, chunk * size), end, place, 0)


def turn_kernel(one_ref, two_ref, one_turned_ref, two_turned_ref):
    one_turned_ref[...] = one_ref[...].T
    two_turned_ref[...] = two_ref[...].T


def first_kernel(
    own_ref,
    across_ref,
    pair_ref,
    own_swap_ref,
    across_swap_ref,
    pair_swap_ref,
    block_ref,
    out_ref,
    full,
):
    width, nodes = own_ref.shape
    odd = lax.axis_index("rep") % 2 == 1
    feat = lax.axis_index("feat")
    core = feat % 2
    quarter = nodes // 4
    half = nodes // 2

    def keep(value, owner):
        row = pl.multiple_of(owner * width, width)
        for part in range(4):
            lane = pl.multiple_of(
                jnp.bitwise_xor(part % 2, core) * half + (part // 2) * quarter, quarter
            )
            full[pl.ds(row, width), pl.ds(lane, quarter)] = value[
                :, part * quarter : (part + 1) * quarter
            ]

    keep(jnp.where(odd, across_ref[...], own_ref[...]), feat)
    keep(jnp.where(odd, across_swap_ref[...], own_swap_ref[...]), jnp.bitwise_xor(feat, 1))
    keep(pair_ref[...], jnp.bitwise_xor(feat, 2))
    keep(pair_swap_ref[...], jnp.bitwise_xor(feat, 3))
    out_ref[...] = dot_nt(full[...], block_ref[:half, :]).astype(out_ref.dtype)


def forward_kernel(own_ref, other_ref, block_ref, out_ref):
    half = own_ref.shape[1]
    total = dot_nt(own_ref[...], block_ref[:half, :half])
    total += dot_nt(other_ref[...], block_ref[:half, half:])
    out_ref[...] = total.astype(out_ref.dtype)


def backward_kernel(own_ref, other_ref, block_ref, out_ref):
    half = own_ref.shape[1]
    total = dot_nn(own_ref[...], block_ref[:half, :half])
    total += dot_nn(other_ref[...], block_ref[half:, :half])
    out_ref[...] = total.astype(out_ref.dtype)


def summed(own_ref, near_ref, across_ref):
    odd = lax.axis_index("rep") % 2 == 1
    second = jnp.where(odd, across_ref[...], own_ref[...])
    return (near_ref[...].astype(jnp.float32) + second.astype(jnp.float32)).astype(jnp.bfloat16)


def slope(value):
    part = jax.nn.sigmoid(value)
    return part * (1.0 + value * (1.0 - part))


def layer_one_kernel(own_ref, near_ref, across_ref, turned_ref, mix_ref, h_ref):
    mix = summed(own_ref, near_ref, across_ref)
    mix_ref[...] = mix
    z = dot_nn(turned_ref[...], mix)
    h_ref[...] = (z * jax.nn.sigmoid(z)).astype(h_ref.dtype)


def layer_two_kernel(
    own_ref,
    near_ref,
    turned_ref,
    weight_ref,
    cot_ref,
    cot_pair_ref,
    mix_ref,
    dz_ref,
    dm_ref,
):
    total = own_ref[...].astype(jnp.float32) + near_ref[...].astype(jnp.float32)
    mix = total.astype(jnp.bfloat16)
    mix_ref[...] = mix
    rate = slope(dot_nn(turned_ref[...], mix))
    upper = lax.axis_index("feat") // 2 == 1
    mine, pair = cot_ref[...], cot_pair_ref[...]
    quarter = mine.shape[1]
    low, high = jnp.where(upper, pair, mine), jnp.where(upper, mine, pair)
    dz_ref[:, :quarter] = (low.astype(jnp.float32) * rate[:, :quarter]).astype(jnp.bfloat16)
    dz_ref[:, quarter:] = (high.astype(jnp.float32) * rate[:, quarter:]).astype(jnp.bfloat16)
    dm_ref[...] = dot_nn(weight_ref[...], dz_ref[...]).astype(dm_ref.dtype)


def slope_kernel(mix_ref, across_ref, turned_ref, here_ref, slope_ref):
    odd = lax.axis_index("rep") % 2 == 1
    mix = jnp.where(odd, across_ref[...], mix_ref[...])
    here_ref[...] = mix
    slope_ref[...] = slope(dot_nn(turned_ref[...], mix))


def grad_kernel(mix_ref, slope_ref, out_ref):
    out_ref[...] = dot_nt(mix_ref[...], slope_ref[...])


def back_one_kernel(own_ref, near_ref, across_ref, slope_ref, dz_ref):
    dh = summed(own_ref, near_ref, across_ref)
    dz_ref[...] = (dh.astype(jnp.float32) * slope_ref[...]).astype(dz_ref.dtype)


def message_kernel(
    dz_ref,
    dz_swap_ref,
    weight_ref,
    block_ref,
    mix_ref,
    mix_swap_ref,
    two_ref,
    two_swap_ref,
    out_ref,
):
    feat = lax.axis_index("feat")
    width = out_ref.shape[0] // 2
    hidden = weight_ref.shape[0]
    half = dz_ref.shape[1]
    mix, mix_swap, dz, dz_swap = mix_ref[...], mix_swap_ref[...], dz_ref[...], dz_swap_ref[...]
    rows = weight_ref[pl.ds(pl.multiple_of(feat * width, width), width), :]
    own = dot_nn(rows, dz).astype(jnp.bfloat16)
    other = dot_nn(rows, dz_swap).astype(jnp.bfloat16)
    total = dot_nn(own, block_ref[:half, :]) + dot_nn(other, block_ref[half:, :])
    out_ref[:width, :] = total.astype(out_ref.dtype)
    swap = feat % 2 == 1
    one = dot_nt(jnp.where(swap, mix_swap, mix), jnp.where(swap, dz_swap, dz)) + dot_nt(
        jnp.where(swap, mix, mix_swap), jnp.where(swap, dz, dz_swap)
    )
    two = two_ref[...] + two_swap_ref[...]
    count = hidden // width
    for index, grad in enumerate((one, two)):
        grad = grad.astype(out_ref.dtype)
        for part in range(count):
            lane = (index * count + part) * hidden
            out_ref[width:, lane : lane + hidden] = grad[part * width : (part + 1) * width, :]


def near_kernel(own_ref, near_ref, across_ref, out_ref):
    out_ref[...] = summed(own_ref, near_ref, across_ref)


def last_kernel(scale, own_ref, far_ref, one_ref, two_ref, out_ref):
    core = lax.axis_index("feat") % 2
    width, nodes = out_ref.shape
    hidden = one_ref.shape[0]
    quarter = nodes // 4
    half = nodes // 2
    for part in range(4):
        lane = pl.multiple_of(
            jnp.bitwise_xor(part % 2, core) * half + (part // 2) * quarter, quarter
        )
        columns = pl.ds(lane, quarter)
        out_ref[:, part * quarter : (part + 1) * quarter] = (
            own_ref[:width, columns] + far_ref[:width, columns]
        )
    count = hidden // width
    for index, grad_ref in enumerate((one_ref, two_ref)):
        for part in range(count):
            lane = (index * count + part) * hidden
            total = own_ref[width:, lane : lane + hidden].astype(jnp.float32)
            total += far_ref[width:, lane : lane + hidden].astype(jnp.float32)
            grad_ref[part * width : (part + 1) * width, :] = total * scale


def paired_shards(
    features, tile_values, tile_coords, section_counts, weight_one, weight_two, cotangent
):
    hidden = weight_one.shape[0]
    width, nodes = features.shape
    side = tile_values.shape[-1]
    panels = nodes // side
    half = nodes // 2
    scale = 1.0 / math.sqrt(nodes * lax.axis_size("loop"))
    product_flops = 2 * hidden * nodes * half

    across = routed(features, to_other_loop)
    pair = routed(features, to_feature_pair)
    own_swap = routed(features, to_other_core)
    (block,) = local_call(
        functools.partial(place_kernel, panels, side),
        [bf16_array(nodes, nodes)],
        [section_counts[0, 0]]
        + [
            pltpu.with_memory_space_constraint(value, pltpu.HBM)
            for value in (tile_coords, tile_values)
        ],
        [pltpu.SMEM, pltpu.HBM, pltpu.HBM],
        [
            pltpu.SMEM(tile_coords.shape, jnp.int32),
            pltpu.VMEM((panels * panels, side, side), jnp.bfloat16),
            pltpu.SemaphoreType.DMA,
            pltpu.SemaphoreType.DMA((4,)),
        ],
        flops=4_000_000_000,
    )
    one_turned, two_turned = local_call(
        turn_kernel,
        [bf16_array(hidden, hidden)] * 2,
        [weight_one, lax.optimization_barrier((weight_two, block))[0]],
    )
    across, pair, block = lax.optimization_barrier((across, pair, block))
    (part_one,) = local_call(
        first_kernel,
        [bf16_array(hidden, half)],
        [
            features,
            across,
            pair,
            own_swap,
            routed(across, to_other_core),
            routed(pair, to_other_core),
            block,
        ],
        None,
        [pltpu.VMEM((hidden, nodes), jnp.bfloat16)],
        flops=product_flops,
    )
    near_one = routed(part_one, to_row_owner)
    across_one = routed(part_one, to_odd_across)
    mix_one, h_one = local_call(
        layer_one_kernel,
        [bf16_array(hidden, half)] * 2,
        [part_one, near_one, across_one, one_turned],
        None,
    )
    (part_two,) = local_call(
        forward_kernel,
        [bf16_array(hidden, half)],
        [h_one, routed(h_one, to_other_core), block],
        flops=product_flops,
    )
    cot_pair = routed(lax.optimization_barrier((cotangent, h_one))[0], to_other_pair)
    near_two, cot_pair = lax.optimization_barrier((routed(part_two, to_other_rep), cot_pair))
    mix_two, dz_two, dm_two = local_call(
        layer_two_kernel,
        [bf16_array(hidden, half)] * 3,
        [part_two, near_two, two_turned, weight_two, cotangent, cot_pair],
        None,
    )
    mix_across = routed(lax.optimization_barrier((mix_one, part_two))[0], to_odd_across)
    dm_swap, mix_across = lax.optimization_barrier((routed(dm_two, to_other_core), mix_across))
    (part_three,) = local_call(
        backward_kernel,
        [bf16_array(hidden, half)],
        [dm_two, dm_swap, block],
        flops=product_flops,
    )
    (grad_two,) = local_call(
        grad_kernel,
        [f32_array(hidden, hidden)],
        [lax.optimization_barrier((mix_two, part_three))[0], dz_two],
    )
    mix_here, slope_here = local_call(
        slope_kernel,
        [bf16_array(hidden, half), f32_array(hidden, half)],
        [mix_one, lax.optimization_barrier((mix_across, part_three))[0], one_turned],
        None,
    )
    near_three, across_three, grad_two_swap, mix_swap = lax.optimization_barrier(
        (
            routed(part_three, to_column_owner),
            routed(part_three, to_odd_across),
            routed(grad_two, to_other_core),
            routed(mix_here, to_other_core),
        )
    )
    (dz_one,) = local_call(
        back_one_kernel,
        [bf16_array(hidden, half)],
        [part_three, near_three, across_three, slope_here],
    )
    (message,) = local_call(
        message_kernel,
        [bf16_array(2 * width, nodes)],
        [
            dz_one,
            routed(dz_one, to_other_core),
            weight_one,
            block,
            mix_here,
            mix_swap,
            grad_two,
            grad_two_swap,
        ],
        None,
        flops=product_flops,
    )
    (near_sum,) = local_call(
        near_kernel,
        [bf16_array(2 * width, nodes)],
        [message, routed(message, to_column_owner), routed(message, to_odd_across)],
    )
    return tuple(
        local_call(
            functools.partial(last_kernel, scale),
            [f32_array(hidden, hidden), f32_array(hidden, hidden), bf16_array(width, nodes)],
            [near_sum, routed(near_sum, to_far_rep, True)],
        )
    )


def solution(mesh):
    sizes = dict(mesh.shape)
    paired = sizes["loop"] == 2 and sizes["rep"] == 4 and sizes["feat"] == 4
    return jax.shard_map(
        paired_shards if paired else ring_shards,
        mesh=mesh,
        in_specs=(
            P("feat", "loop"),
            P("loop", "rep", None, None, None),
            P("loop", "rep", None, None),
            P("loop", "rep", None),
            P(),
            P(),
            P(None, ("loop", "feat")),
        ),
        out_specs=(P(), P(), P("feat", "loop")),
        check_vma=False,
    )
```

```python
import functools
import math

import jax
import jax.numpy as jnp
from jax import lax
from jax.experimental import pallas as pl
from jax.experimental.pallas import tpu as pltpu
from jax.sharding import PartitionSpec as P

tile_batch = 8


def shortened(shard):

    def short(part):
        return part.astype(jnp.bfloat16) if part.dtype == jnp.float32 else part

    return jax.tree.map(short, shard)


def passed_along(value, axis, steps):
    count = lax.axis_size(axis)
    pairs = [(source, (source + steps) % count) for source in range(count)]
    return lax.ppermute(value, axis, pairs)


def silu_slope(argument):
    sigmoid_value = jax.nn.sigmoid(argument)
    return sigmoid_value * (1.0 + argument * (1.0 - sigmoid_value))


def section_term(source, section_id, layout, transposed, enabled=True):
    tile_set, row_ids, col_ids, starts, filled, panels = layout
    feat_width = source.shape[0]
    tile_side = tile_set.shape[-1]
    slot_total = tile_set.shape[0]
    shaped = source.reshape(feat_width, panels, tile_side)
    first = starts[section_id]
    number = jnp.where(enabled, filled[section_id], 0)
    rounds = (number + tile_batch - 1) // tile_batch
    offsets = jnp.arange(tile_batch, dtype=jnp.int32)
    panel_ids = jnp.arange(panels, dtype=jnp.int32)

    def one_round(round_id, running):
        within = round_id * tile_batch + offsets
        alive_mask = within < number
        slot_ids = jnp.minimum(first + within, slot_total - 1)
        chosen = tile_set[slot_ids]
        if transposed:
            picked = shaped[:, row_ids[slot_ids], :]
            products = jnp.einsum(
                "dba,bac->dbc", picked, chosen, preferred_element_type=jnp.float32
            )
            target = col_ids[slot_ids]
        else:
            picked = shaped[:, col_ids[slot_ids], :]
            products = jnp.einsum(
                "dbc,bac->dba", picked, chosen, preferred_element_type=jnp.float32
            )
            target = row_ids[slot_ids]
        placing = ((target[:, None] == panel_ids[None, :]) & alive_mask[:, None]).astype(
            jnp.float32
        )
        return running + jnp.einsum(
            "dbe,bp->dpe", products, placing, precision=lax.Precision.HIGHEST
        )

    zero_block = jnp.zeros((feat_width, panels, tile_side), jnp.float32)
    return lax.fori_loop(0, rounds, one_round, zero_block).reshape(feat_width, panels * tile_side)


def advance(block, stride):
    return jax.tree.map(
        lambda part, own: part.astype(own.dtype),
        passed_along(shortened(block), "loop", stride),
        block,
    )


def forward_product(source, layout):
    loop_size = lax.axis_size("loop")
    rep_size = lax.axis_size("rep")
    rep_index = lax.axis_index("rep")
    sections = -(-loop_size // rep_size)
    stride = rep_size % loop_size
    current = source
    for bit in range(rep_size.bit_length() - 1):
        jump = (1 << bit) % loop_size
        if jump:
            moved = passed_along(current, "loop", jump)
            current = jnp.where((rep_index >> bit) % 2 == 1, moved, current)
    running = section_term(current, 0, layout, False)
    if sections > 1:

        def onward(step_id, carry):
            ahead, acc = carry
            ahead = advance(ahead, stride)
            return (ahead, acc + section_term(ahead, step_id, layout, False))

        ahead, running = lax.fori_loop(1, sections, onward, (current, running))
    return running


def transposed_product(source, layout):
    loop_size = lax.axis_size("loop")
    rep_size = lax.axis_size("rep")
    rep_index = lax.axis_index("rep")
    sections = -(-loop_size // rep_size)
    stride = rep_size % loop_size
    running = section_term(source, sections - 1, layout, True)
    if sections > 1:

        def backward(step_id, acc):
            acc = jax.tree.map(
                lambda part, own: part.astype(own.dtype),
                passed_along(shortened(acc), "loop", -stride),
                acc,
            )
            return acc + section_term(source, sections - 1 - step_id, layout, True)

        running = lax.fori_loop(1, sections, backward, running)
    for bit in range(rep_size.bit_length() - 1):
        jump = (1 << bit) % loop_size
        if jump:
            moved = passed_along(running.astype(jnp.bfloat16), "loop", -jump).astype(running.dtype)
            running = jnp.where((rep_index >> bit) % 2 == 1, moved, running)
    return running


def to_nodes(partial_value):
    summed = lax.psum(partial_value.astype(jnp.bfloat16), "rep")
    return lax.all_to_all(summed, "feat", split_axis=1, concat_axis=0, tiled=True)


def to_features(node_block):
    return lax.all_to_all(node_block, "feat", split_axis=0, concat_axis=1, tiled=True)


def weight_grad(mixed, slope):
    part_sum = jnp.einsum("dq,eq->de", mixed, slope, preferred_element_type=jnp.float32)
    return lax.psum(part_sum, ("loop", "feat"))


def ring_shards(features, tile_values, tile_coords, section_counts, weight_one, weight_two, cotangent):
    tile_set = tile_values[0, 0]
    row_ids = tile_coords[0, 0, 0]
    col_ids = tile_coords[0, 0, 1]
    filled = section_counts[0, 0]
    starts = jnp.cumsum(filled) - filled
    panels = features.shape[1] // tile_set.shape[-1]
    layout = (tile_set, row_ids, col_ids, starts, filled, panels)
    scale = 1.0 / math.sqrt(features.shape[1] * lax.axis_size("loop"))
    mix_one = to_nodes(forward_product(features, layout))
    z_one = jnp.einsum("de,dq->eq", weight_one, mix_one, preferred_element_type=jnp.float32)
    h_one = jax.nn.silu(z_one).astype(jnp.bfloat16)
    mix_two = to_nodes(forward_product(to_features(h_one), layout))
    z_two = jnp.einsum("de,dq->eq", weight_two, mix_two, preferred_element_type=jnp.float32)
    dz_two = (cotangent * silu_slope(z_two)).astype(jnp.bfloat16)
    grad_two = weight_grad(mix_two, dz_two) * scale
    dm_two = jnp.einsum("de,eq->dq", weight_two, dz_two, preferred_element_type=jnp.float32).astype(
        jnp.bfloat16
    )
    dh_one = to_nodes(transposed_product(to_features(dm_two), layout))
    dz_one = (dh_one * silu_slope(z_one)).astype(jnp.bfloat16)
    grad_one = weight_grad(mix_one, dz_one) * scale
    dm_one = jnp.einsum("de,eq->dq", weight_one, dz_one, preferred_element_type=jnp.float32).astype(
        jnp.bfloat16
    )
    partial_value = transposed_product(to_features(dm_one), layout)
    input_grad = lax.psum(partial_value.astype(jnp.bfloat16), "rep")
    return (grad_one, grad_two, input_grad)


mesh_axes = ("loop", "rep", "feat")
vmem_bytes = 24 * 1024 * 1024


def routed(value, target, outward=False):
    loops, reps, feats = (lax.axis_size(axis) for axis in mesh_axes)
    pairs = []
    for i in range(loops):
        for r in range(reps):
            for f in range(feats):
                idle = r >= loops
                if idle and outward:
                    continue
                to_loop, to_rep, to_feat = to_other_core(i, r, f) if idle else target(i, r, f)
                pairs.append(
                    ((i * reps + r) * feats + f, (to_loop * reps + to_rep) * feats + to_feat)
                )
    return lax.ppermute(value, mesh_axes, pairs)


def to_other_core(i, r, f):
    return i, r, f ^ 1


def to_other_pair(i, r, f):
    return i, r, f ^ 2


def to_other_loop(i, r, f):
    return 1 - i, r, f


def to_odd_across(i, r, f):
    return (1 - i, r, f) if r % 2 else (i, r, f ^ 1)


def to_other_rep(i, r, f):
    return i, r ^ 1, f


def to_row_owner(i, r, f):
    return (i, r - 1, f) if r % 2 else (1 - i, r + 1, f)


def to_column_owner(i, r, f):
    return (1 - i, r - 1, f) if r % 2 else (i, r + 1, f)


def to_far_rep(i, r, f):
    return i, r ^ 2, f


def to_far_column_owner(i, r, f):
    return (1 - i if r % 2 else i), r ^ 2, f


def to_last_column_owner(i, r, f):
    return (1 - i if r % 2 else i), r ^ 3, f


def to_feature_pair(i, r, f):
    return (1 - i if r % 2 else i), r, f ^ 2


def local_call(kernel, outs, operands, spaces=None, scratch=(), flops=0):
    spaces = spaces or [pltpu.VMEM] * len(operands)
    moved = sum(o.size * o.dtype.itemsize for o in operands) + sum(
        math.prod(o.shape) * 4 for o in outs
    )
    return pl.pallas_call(
        kernel,
        out_shape=list(outs),
        in_specs=[pl.BlockSpec(memory_space=space) for space in spaces],
        out_specs=[pl.BlockSpec(memory_space=pltpu.VMEM) for _ in outs],
        scratch_shapes=list(scratch),
        compiler_params=pltpu.CompilerParams(vmem_limit_bytes=vmem_bytes),
        cost_estimate=pl.CostEstimate(flops=flops, bytes_accessed=moved, transcendentals=0),
    )(*operands)


def bf16_array(*shape):
    return jax.ShapeDtypeStruct(shape, jnp.bfloat16)


def f32_array(*shape):
    return jax.ShapeDtypeStruct(shape, jnp.float32)


def dot_nn(a, b):
    return lax.dot_general(a, b, (((1,), (0,)), ((), ())), preferred_element_type=jnp.float32)


def dot_nt(a, b):
    return lax.dot_general(a, b, (((1,), (1,)), ((), ())), preferred_element_type=jnp.float32)


def place_kernel(
    panels,
    side,
    count_ref,
    coords_ref,
    tiles_ref,
    block_ref,
    starts,
    coords,
    held,
    list_sem,
    sems,
):
    chunks = sems.shape[0]
    size = held.shape[0] // chunks
    lists = pltpu.make_async_copy(coords_ref, coords, list_sem)
    lists.start()
    copies = []
    for chunk in range(chunks):
        here = pl.ds(chunk * size, size)
        copies.append(
            pltpu.make_async_copy(tiles_ref.at[0, 0, here], held.at[here], sems.at[chunk])
        )
        copies[-1].start()
    block_ref[...] = jnp.zeros_like(block_ref)
    quarter = panels // 4
    core = lax.axis_index("feat") % 2
    lists.wait()
    count = count_ref[0]

    for panel in range(panels):
        part, rest = divmod(panel, quarter)
        first = ((part % 2) * 2 + part // 2) * quarter + rest
        second = ((1 - part % 2) * 2 + part // 2) * quarter + rest
        starts[panel] = jnp.where(core == 0, first, second) * side

    def start_of(panel):
        return pl.multiple_of(starts[panel], side)

    def place(slot, carry):
        rows = pl.ds(start_of(coords[0, 0, 0, slot]), side)
        columns = pl.ds(start_of(coords[0, 0, 1, slot]), side)
        block_ref[rows, columns] = held[slot]
        return carry

    group = 8

    def place_group(index, carry):
        for offset in range(group):
            place(index * group + offset, carry)
        return carry

    for chunk in range(chunks):
        copies[chunk].wait()
        end = jnp.minimum(count, (chunk + 1) * size)
        whole = end // group
        lax.fori_loop(chunk * size // group, whole, place_group, 0)
        lax.fori_loop(jnp.maximum(whole * group, chunk * size), end, place, 0)


def turn_kernel(one_ref, two_ref, one_turned_ref, two_turned_ref):
    one_turned_ref[...] = one_ref[...].T
    two_turned_ref[...] = two_ref[...].T


def first_kernel(
    own_ref,
    across_ref,
    pair_ref,
    own_swap_ref,
    across_swap_ref,
    pair_swap_ref,
    block_ref,
    out_ref,
    full,
):
    width, nodes = own_ref.shape
    odd = lax.axis_index("rep") % 2 == 1
    feat = lax.axis_index("feat")
    core = feat % 2
    quarter = nodes // 4
    half = nodes // 2

    def keep(value, owner):
        row = pl.multiple_of(owner * width, width)
        for part in range(4):
            lane = pl.multiple_of(
                jnp.bitwise_xor(part % 2, core) * half + (part // 2) * quarter, quarter
            )
            full[pl.ds(row, width), pl.ds(lane, quarter)] = value[
                :, part * quarter : (part + 1) * quarter
            ]

    keep(jnp.where(odd, across_ref[...], own_ref[...]), feat)
    keep(jnp.where(odd, across_swap_ref[...], own_swap_ref[...]), jnp.bitwise_xor(feat, 1))
    keep(pair_ref[...], jnp.bitwise_xor(feat, 2))
    keep(pair_swap_ref[...], jnp.bitwise_xor(feat, 3))
    out_ref[...] = dot_nt(full[...], block_ref[:half, :]).astype(out_ref.dtype)


def forward_own_kernel(own_ref, block_ref, total_ref):
    half = own_ref.shape[1]
    total_ref[...] = dot_nt(own_ref[...], block_ref[:half, :half])


def forward_other_kernel(total_ref, other_ref, block_ref, out_ref):
    half = other_ref.shape[1]
    total = total_ref[...] + dot_nt(other_ref[...], block_ref[:half, half:])
    out_ref[...] = total.astype(out_ref.dtype)


def backward_own_kernel(own_ref, block_ref, total_ref):
    half = own_ref.shape[1]
    total_ref[...] = dot_nn(own_ref[...], block_ref[:half, :half])


def backward_other_kernel(total_ref, other_ref, block_ref, out_ref):
    half = other_ref.shape[1]
    total = total_ref[...] + dot_nn(other_ref[...], block_ref[half:, :half])
    out_ref[...] = total.astype(out_ref.dtype)


def summed(own_ref, near_ref, across_ref):
    odd = lax.axis_index("rep") % 2 == 1
    second = jnp.where(odd, across_ref[...], own_ref[...])
    return (near_ref[...].astype(jnp.float32) + second.astype(jnp.float32)).astype(jnp.bfloat16)


def slope(value):
    part = jax.nn.sigmoid(value)
    return part * (1.0 + value * (1.0 - part))


def layer_one_kernel(own_ref, near_ref, across_ref, turned_ref, mix_ref, h_ref):
    mix = summed(own_ref, near_ref, across_ref)
    mix_ref[...] = mix
    z = dot_nn(turned_ref[...], mix)
    h_ref[...] = (z * jax.nn.sigmoid(z)).astype(h_ref.dtype)


def layer_two_kernel(
    own_ref,
    near_ref,
    turned_ref,
    weight_ref,
    cot_ref,
    cot_pair_ref,
    mix_ref,
    dz_ref,
    dm_ref,
):
    total = own_ref[...].astype(jnp.float32) + near_ref[...].astype(jnp.float32)
    mix = total.astype(jnp.bfloat16)
    mix_ref[...] = mix
    rate = slope(dot_nn(turned_ref[...], mix))
    upper = lax.axis_index("feat") // 2 == 1
    mine, pair = cot_ref[...], cot_pair_ref[...]
    quarter = mine.shape[1]
    low, high = jnp.where(upper, pair, mine), jnp.where(upper, mine, pair)
    dz_ref[:, :quarter] = (low.astype(jnp.float32) * rate[:, :quarter]).astype(jnp.bfloat16)
    dz_ref[:, quarter:] = (high.astype(jnp.float32) * rate[:, quarter:]).astype(jnp.bfloat16)
    dm_ref[...] = dot_nn(weight_ref[...], dz_ref[...]).astype(dm_ref.dtype)


def slope_kernel(mix_ref, across_ref, turned_ref, here_ref, slope_ref):
    odd = lax.axis_index("rep") % 2 == 1
    mix = jnp.where(odd, across_ref[...], mix_ref[...])
    here_ref[...] = mix
    slope_ref[...] = slope(dot_nn(turned_ref[...], mix))


def grad_kernel(mix_ref, slope_ref, out_ref):
    out_ref[...] = dot_nt(mix_ref[...], slope_ref[...])


def back_one_kernel(own_ref, near_ref, across_ref, slope_ref, dz_ref):
    dh = summed(own_ref, near_ref, across_ref)
    dz_ref[...] = (dh.astype(jnp.float32) * slope_ref[...]).astype(dz_ref.dtype)


def feature_rows(weight_ref, width):
    first = pl.multiple_of(lax.axis_index("feat") * width, width)
    return weight_ref[pl.ds(first, width), :]


def last_own_kernel(dz_ref, weight_ref, block_ref, mix_ref, total_ref, grad_ref):
    half = dz_ref.shape[1]
    own = dot_nn(feature_rows(weight_ref, total_ref.shape[0]), dz_ref[...]).astype(jnp.bfloat16)
    total_ref[...] = dot_nn(own, block_ref[:half, :])
    grad_ref[...] = dot_nt(mix_ref[...], dz_ref[...])


def message_kernel(
    total_ref,
    grad_ref,
    dz_swap_ref,
    weight_ref,
    block_ref,
    mix_swap_ref,
    two_ref,
    two_swap_ref,
    out_ref,
):
    width = total_ref.shape[0]
    hidden = weight_ref.shape[0]
    half = dz_swap_ref.shape[1]
    dz_swap = dz_swap_ref[...]
    other = dot_nn(feature_rows(weight_ref, width), dz_swap).astype(jnp.bfloat16)
    total = total_ref[...] + dot_nn(other, block_ref[half:, :])
    out_ref[:width, :] = total.astype(out_ref.dtype)
    second = lax.axis_index("feat") % 2 == 1
    grad, grad_swap = grad_ref[...], dot_nt(mix_swap_ref[...], dz_swap)
    one = jnp.where(second, grad_swap, grad) + jnp.where(second, grad, grad_swap)
    two = two_ref[...] + two_swap_ref[...]
    count = hidden // width
    for index, grad in enumerate((one, two)):
        grad = grad.astype(out_ref.dtype)
        for part in range(count):
            lane = (index * count + part) * hidden
            out_ref[width:, lane : lane + hidden] = grad[part * width : (part + 1) * width, :]


def near_kernel(own_ref, near_ref, across_ref, out_ref):
    out_ref[...] = summed(own_ref, near_ref, across_ref)


def last_kernel(scale, own_ref, far_ref, one_ref, two_ref, out_ref):
    core = lax.axis_index("feat") % 2
    width, nodes = out_ref.shape
    hidden = one_ref.shape[0]
    quarter = nodes // 4
    half = nodes // 2
    for part in range(4):
        lane = pl.multiple_of(
            jnp.bitwise_xor(part % 2, core) * half + (part // 2) * quarter, quarter
        )
        columns = pl.ds(lane, quarter)
        out_ref[:, part * quarter : (part + 1) * quarter] = (
            own_ref[:width, columns] + far_ref[:width, columns]
        )
    count = hidden // width
    for index, grad_ref in enumerate((one_ref, two_ref)):
        for part in range(count):
            lane = (index * count + part) * hidden
            total = own_ref[width:, lane : lane + hidden].astype(jnp.float32)
            total += far_ref[width:, lane : lane + hidden].astype(jnp.float32)
            grad_ref[part * width : (part + 1) * width, :] = total * scale


def paired_shards(
    features, tile_values, tile_coords, section_counts, weight_one, weight_two, cotangent
):
    hidden = weight_one.shape[0]
    width, nodes = features.shape
    side = tile_values.shape[-1]
    panels = nodes // side
    half = nodes // 2
    scale = 1.0 / math.sqrt(nodes * lax.axis_size("loop"))
    product_flops = 2 * hidden * nodes * half

    across = routed(features, to_odd_across)
    pair = routed(features, to_feature_pair)
    own_swap = routed(features, to_other_core)
    (block,) = local_call(
        functools.partial(place_kernel, panels, side),
        [bf16_array(nodes, nodes)],
        [section_counts[0, 0]]
        + [
            pltpu.with_memory_space_constraint(value, pltpu.HBM)
            for value in (tile_coords, tile_values)
        ],
        [pltpu.SMEM, pltpu.HBM, pltpu.HBM],
        [
            pltpu.SMEM((panels,), jnp.int32),
            pltpu.SMEM(tile_coords.shape, jnp.int32),
            pltpu.VMEM((panels * panels, side, side), jnp.bfloat16),
            pltpu.SemaphoreType.DMA,
            pltpu.SemaphoreType.DMA((4,)),
        ],
        flops=4_000_000_000,
    )
    one_turned, two_turned = local_call(
        turn_kernel,
        [bf16_array(hidden, hidden)] * 2,
        [weight_one, lax.optimization_barrier((weight_two, block))[0]],
    )
    across, pair, block = lax.optimization_barrier((across, pair, block))
    (part_one,) = local_call(
        first_kernel,
        [bf16_array(hidden, half)],
        [
            features,
            across,
            pair,
            own_swap,
            routed(across, to_other_core),
            routed(pair, to_other_core),
            block,
        ],
        None,
        [pltpu.VMEM((hidden, nodes), jnp.bfloat16)],
        flops=product_flops,
    )
    near_one = routed(part_one, to_row_owner)
    across_one = routed(part_one, to_odd_across)
    mix_one, h_one = local_call(
        layer_one_kernel,
        [bf16_array(hidden, half)] * 2,
        [part_one, near_one, across_one, one_turned],
        None,
    )
    h_swap = routed(h_one, to_other_core)
    (total_two,) = local_call(
        forward_own_kernel, [f32_array(hidden, half)], [h_one, block], flops=product_flops // 2
    )
    (part_two,) = local_call(
        forward_other_kernel,
        [bf16_array(hidden, half)],
        [total_two, h_swap, block],
        flops=product_flops // 2,
    )
    cot_pair = routed(lax.optimization_barrier((cotangent, h_one))[0], to_other_pair)
    near_two, cot_pair = lax.optimization_barrier((routed(part_two, to_other_rep), cot_pair))
    mix_two, dz_two, dm_two = local_call(
        layer_two_kernel,
        [bf16_array(hidden, half)] * 3,
        [part_two, near_two, two_turned, weight_two, cotangent, cot_pair],
        None,
    )
    mix_across = routed(lax.optimization_barrier((mix_one, part_two))[0], to_odd_across)
    mix_here, slope_here = local_call(
        slope_kernel,
        [bf16_array(hidden, half), f32_array(hidden, half)],
        [mix_one, lax.optimization_barrier((mix_across, dm_two))[0], one_turned],
    )
    (total_three,) = local_call(
        backward_own_kernel, [f32_array(hidden, half)], [dm_two, block], flops=product_flops // 2
    )
    dm_swap, slope_here, total_three = lax.optimization_barrier(
        (routed(dm_two, to_other_core), slope_here, total_three)
    )
    (part_three,) = local_call(
        backward_other_kernel,
        [bf16_array(hidden, half)],
        [total_three, dm_swap, block],
        flops=product_flops // 2,
    )
    (grad_two,) = local_call(
        grad_kernel,
        [f32_array(hidden, hidden)],
        [lax.optimization_barrier((mix_two, part_three))[0], dz_two],
    )
    near_three, across_three, grad_two_swap, mix_swap = lax.optimization_barrier(
        (
            routed(part_three, to_column_owner),
            routed(part_three, to_odd_across),
            routed(grad_two, to_other_core),
            routed(mix_here, to_other_core),
        )
    )
    (dz_one,) = local_call(
        back_one_kernel,
        [bf16_array(hidden, half)],
        [part_three, near_three, across_three, slope_here],
    )
    dz_swap = routed(dz_one, to_other_core)
    total_four, grad_one = local_call(
        last_own_kernel,
        [f32_array(width, nodes), f32_array(hidden, hidden)],
        [dz_one, weight_one, block, mix_here],
        flops=product_flops // 2,
    )
    dz_swap, total_four = lax.optimization_barrier((dz_swap, total_four))
    (message,) = local_call(
        message_kernel,
        [bf16_array(2 * width, nodes)],
        [
            total_four,
            grad_one,
            dz_swap,
            weight_one,
            block,
            mix_swap,
            grad_two,
            grad_two_swap,
        ],
        flops=product_flops // 2,
    )
    (near_sum,) = local_call(
        near_kernel,
        [bf16_array(2 * width, nodes)],
        [message, routed(message, to_column_owner), routed(message, to_odd_across)],
    )
    return tuple(
        local_call(
            functools.partial(last_kernel, scale),
            [f32_array(hidden, hidden), f32_array(hidden, hidden), bf16_array(width, nodes)],
            [near_sum, routed(near_sum, to_far_rep, True)],
        )
    )


def solution(mesh):
    sizes = dict(mesh.shape)
    paired = sizes["loop"] == 2 and sizes["rep"] == 4 and sizes["feat"] == 4
    return jax.shard_map(
        paired_shards if paired else ring_shards,
        mesh=mesh,
        in_specs=(
            P("feat", "loop"),
            P("loop", "rep", None, None, None),
            P("loop", "rep", None, None),
            P("loop", "rep", None),
            P(),
            P(),
            P(None, ("loop", "feat")),
        ),
        out_specs=(P(), P(), P("feat", "loop")),
        check_vma=False,
    )
```

```python
import functools
import math

import jax
import jax.numpy as jnp
from jax import lax
from jax.experimental import pallas as pl
from jax.experimental.pallas import tpu as pltpu
from jax.sharding import PartitionSpec as P

tile_batch = 8


def shortened(shard):

    def short(part):
        return part.astype(jnp.bfloat16) if part.dtype == jnp.float32 else part

    return jax.tree.map(short, shard)


def passed_along(value, axis, steps):
    count = lax.axis_size(axis)
    pairs = [(source, (source + steps) % count) for source in range(count)]
    return lax.ppermute(value, axis, pairs)


def silu_slope(argument):
    sigmoid_value = jax.nn.sigmoid(argument)
    return sigmoid_value * (1.0 + argument * (1.0 - sigmoid_value))


def section_term(source, section_id, layout, transposed, enabled=True):
    tile_set, row_ids, col_ids, starts, filled, panels = layout
    feat_width = source.shape[0]
    tile_side = tile_set.shape[-1]
    slot_total = tile_set.shape[0]
    shaped = source.reshape(feat_width, panels, tile_side)
    first = starts[section_id]
    number = jnp.where(enabled, filled[section_id], 0)
    rounds = (number + tile_batch - 1) // tile_batch
    offsets = jnp.arange(tile_batch, dtype=jnp.int32)
    panel_ids = jnp.arange(panels, dtype=jnp.int32)

    def one_round(round_id, running):
        within = round_id * tile_batch + offsets
        alive_mask = within < number
        slot_ids = jnp.minimum(first + within, slot_total - 1)
        chosen = tile_set[slot_ids]
        if transposed:
            picked = shaped[:, row_ids[slot_ids], :]
            products = jnp.einsum(
                "dba,bac->dbc", picked, chosen, preferred_element_type=jnp.float32
            )
            target = col_ids[slot_ids]
        else:
            picked = shaped[:, col_ids[slot_ids], :]
            products = jnp.einsum(
                "dbc,bac->dba", picked, chosen, preferred_element_type=jnp.float32
            )
            target = row_ids[slot_ids]
        placing = ((target[:, None] == panel_ids[None, :]) & alive_mask[:, None]).astype(
            jnp.float32
        )
        return running + jnp.einsum(
            "dbe,bp->dpe", products, placing, precision=lax.Precision.HIGHEST
        )

    zero_block = jnp.zeros((feat_width, panels, tile_side), jnp.float32)
    return lax.fori_loop(0, rounds, one_round, zero_block).reshape(feat_width, panels * tile_side)


def advance(block, stride):
    return jax.tree.map(
        lambda part, own: part.astype(own.dtype),
        passed_along(shortened(block), "loop", stride),
        block,
    )


def forward_product(source, layout):
    loop_size = lax.axis_size("loop")
    rep_size = lax.axis_size("rep")
    rep_index = lax.axis_index("rep")
    sections = -(-loop_size // rep_size)
    stride = rep_size % loop_size
    current = source
    for bit in range(rep_size.bit_length() - 1):
        jump = (1 << bit) % loop_size
        if jump:
            moved = passed_along(current, "loop", jump)
            current = jnp.where((rep_index >> bit) % 2 == 1, moved, current)
    running = section_term(current, 0, layout, False)
    if sections > 1:

        def onward(step_id, carry):
            ahead, acc = carry
            ahead = advance(ahead, stride)
            return (ahead, acc + section_term(ahead, step_id, layout, False))

        ahead, running = lax.fori_loop(1, sections, onward, (current, running))
    return running


def transposed_product(source, layout):
    loop_size = lax.axis_size("loop")
    rep_size = lax.axis_size("rep")
    rep_index = lax.axis_index("rep")
    sections = -(-loop_size // rep_size)
    stride = rep_size % loop_size
    running = section_term(source, sections - 1, layout, True)
    if sections > 1:

        def backward(step_id, acc):
            acc = jax.tree.map(
                lambda part, own: part.astype(own.dtype),
                passed_along(shortened(acc), "loop", -stride),
                acc,
            )
            return acc + section_term(source, sections - 1 - step_id, layout, True)

        running = lax.fori_loop(1, sections, backward, running)
    for bit in range(rep_size.bit_length() - 1):
        jump = (1 << bit) % loop_size
        if jump:
            moved = passed_along(running.astype(jnp.bfloat16), "loop", -jump).astype(running.dtype)
            running = jnp.where((rep_index >> bit) % 2 == 1, moved, running)
    return running


def to_nodes(partial_value):
    summed = lax.psum(partial_value.astype(jnp.bfloat16), "rep")
    return lax.all_to_all(summed, "feat", split_axis=1, concat_axis=0, tiled=True)


def to_features(node_block):
    return lax.all_to_all(node_block, "feat", split_axis=0, concat_axis=1, tiled=True)


def weight_grad(mixed, slope):
    part_sum = jnp.einsum("dq,eq->de", mixed, slope, preferred_element_type=jnp.float32)
    return lax.psum(part_sum, ("loop", "feat"))


def ring_shards(features, tile_values, tile_coords, section_counts, weight_one, weight_two, cotangent):
    tile_set = tile_values[0, 0]
    row_ids = tile_coords[0, 0, 0]
    col_ids = tile_coords[0, 0, 1]
    filled = section_counts[0, 0]
    starts = jnp.cumsum(filled) - filled
    panels = features.shape[1] // tile_set.shape[-1]
    layout = (tile_set, row_ids, col_ids, starts, filled, panels)
    scale = 1.0 / math.sqrt(features.shape[1] * lax.axis_size("loop"))
    mix_one = to_nodes(forward_product(features, layout))
    z_one = jnp.einsum("de,dq->eq", weight_one, mix_one, preferred_element_type=jnp.float32)
    h_one = jax.nn.silu(z_one).astype(jnp.bfloat16)
    mix_two = to_nodes(forward_product(to_features(h_one), layout))
    z_two = jnp.einsum("de,dq->eq", weight_two, mix_two, preferred_element_type=jnp.float32)
    dz_two = (cotangent * silu_slope(z_two)).astype(jnp.bfloat16)
    grad_two = weight_grad(mix_two, dz_two) * scale
    dm_two = jnp.einsum("de,eq->dq", weight_two, dz_two, preferred_element_type=jnp.float32).astype(
        jnp.bfloat16
    )
    dh_one = to_nodes(transposed_product(to_features(dm_two), layout))
    dz_one = (dh_one * silu_slope(z_one)).astype(jnp.bfloat16)
    grad_one = weight_grad(mix_one, dz_one) * scale
    dm_one = jnp.einsum("de,eq->dq", weight_one, dz_one, preferred_element_type=jnp.float32).astype(
        jnp.bfloat16
    )
    partial_value = transposed_product(to_features(dm_one), layout)
    input_grad = lax.psum(partial_value.astype(jnp.bfloat16), "rep")
    return (grad_one, grad_two, input_grad)


mesh_axes = ("loop", "rep", "feat")
vmem_bytes = 24 * 1024 * 1024


def routed(value, target, outward=False):
    loops, reps, feats = (lax.axis_size(axis) for axis in mesh_axes)
    pairs = []
    for i in range(loops):
        for r in range(reps):
            for f in range(feats):
                idle = r >= loops
                if idle and outward:
                    continue
                to_loop, to_rep, to_feat = to_other_core(i, r, f) if idle else target(i, r, f)
                pairs.append(
                    ((i * reps + r) * feats + f, (to_loop * reps + to_rep) * feats + to_feat)
                )
    return lax.ppermute(value, mesh_axes, pairs)


def to_other_core(i, r, f):
    return i, r, f ^ 1


def to_other_pair(i, r, f):
    return i, r, f ^ 2


def to_other_loop(i, r, f):
    return 1 - i, r, f


def to_odd_across(i, r, f):
    return (1 - i, r, f) if r % 2 else (i, r, f ^ 1)


def to_other_rep(i, r, f):
    return i, r ^ 1, f


def to_row_owner(i, r, f):
    return (i, r - 1, f) if r % 2 else (1 - i, r + 1, f)


def to_column_owner(i, r, f):
    return (1 - i, r - 1, f) if r % 2 else (i, r + 1, f)


def to_far_rep(i, r, f):
    return i, r ^ 2, f


def to_far_column_owner(i, r, f):
    return (1 - i if r % 2 else i), r ^ 2, f


def to_last_column_owner(i, r, f):
    return (1 - i if r % 2 else i), r ^ 3, f


def to_feature_pair(i, r, f):
    return (1 - i if r % 2 else i), r, f ^ 2


def local_call(kernel, outs, operands, spaces=None, scratch=(), flops=0):
    spaces = spaces or [pltpu.VMEM] * len(operands)
    moved = sum(o.size * o.dtype.itemsize for o in operands) + sum(
        math.prod(o.shape) * 4 for o in outs
    )
    return pl.pallas_call(
        kernel,
        out_shape=list(outs),
        in_specs=[pl.BlockSpec(memory_space=space) for space in spaces],
        out_specs=[pl.BlockSpec(memory_space=pltpu.VMEM) for _ in outs],
        scratch_shapes=list(scratch),
        compiler_params=pltpu.CompilerParams(vmem_limit_bytes=vmem_bytes),
        cost_estimate=pl.CostEstimate(flops=flops, bytes_accessed=moved, transcendentals=0),
    )(*operands)


def bf16_array(*shape):
    return jax.ShapeDtypeStruct(shape, jnp.bfloat16)


def f32_array(*shape):
    return jax.ShapeDtypeStruct(shape, jnp.float32)


def dot_nn(a, b):
    return lax.dot_general(a, b, (((1,), (0,)), ((), ())), preferred_element_type=jnp.float32)


def dot_nt(a, b):
    return lax.dot_general(a, b, (((1,), (1,)), ((), ())), preferred_element_type=jnp.float32)


def place_kernel(
    panels,
    side,
    count_ref,
    coords_ref,
    tiles_ref,
    block_ref,
    starts,
    coords,
    held,
    list_sem,
    sems,
):
    chunks = sems.shape[0]
    size = held.shape[0] // chunks
    lists = pltpu.make_async_copy(coords_ref, coords, list_sem)
    lists.start()
    copies = []
    for chunk in range(chunks):
        here = pl.ds(chunk * size, size)
        copies.append(
            pltpu.make_async_copy(tiles_ref.at[0, 0, here], held.at[here], sems.at[chunk])
        )
        copies[-1].start()
    block_ref[...] = jnp.zeros_like(block_ref)
    quarter = panels // 4
    core = lax.axis_index("feat") % 2
    lists.wait()
    count = count_ref[0]

    for panel in range(panels):
        part, rest = divmod(panel, quarter)
        first = ((part % 2) * 2 + part // 2) * quarter + rest
        second = ((1 - part % 2) * 2 + part // 2) * quarter + rest
        starts[panel] = jnp.where(core == 0, first, second) * side

    def start_of(panel):
        return pl.multiple_of(starts[panel], side)

    def place(slot, carry):
        rows = pl.ds(start_of(coords[0, 0, 0, slot]), side)
        columns = pl.ds(start_of(coords[0, 0, 1, slot]), side)
        block_ref[rows, columns] = held[slot]
        return carry

    group = 8

    def place_group(index, carry):
        for offset in range(group):
            place(index * group + offset, carry)
        return carry

    for chunk in range(chunks):
        copies[chunk].wait()
        end = jnp.minimum(count, (chunk + 1) * size)
        whole = end // group
        lax.fori_loop(chunk * size // group, whole, place_group, 0)
        lax.fori_loop(jnp.maximum(whole * group, chunk * size), end, place, 0)


def turn_kernel(one_ref, two_ref, one_turned_ref, two_turned_ref):
    one_turned_ref[...] = one_ref[...].T
    two_turned_ref[...] = two_ref[...].T


def first_kernel(
    own_ref,
    across_ref,
    pair_ref,
    own_swap_ref,
    across_swap_ref,
    pair_swap_ref,
    block_ref,
    out_ref,
    full,
):
    width, nodes = own_ref.shape
    odd = lax.axis_index("rep") % 2 == 1
    feat = lax.axis_index("feat")
    core = feat % 2
    quarter = nodes // 4
    half = nodes // 2

    def keep(value, owner):
        row = pl.multiple_of(owner * width, width)
        for part in range(4):
            lane = pl.multiple_of(
                jnp.bitwise_xor(part % 2, core) * half + (part // 2) * quarter, quarter
            )
            full[pl.ds(row, width), pl.ds(lane, quarter)] = value[
                :, part * quarter : (part + 1) * quarter
            ]

    keep(jnp.where(odd, across_ref[...], own_ref[...]), feat)
    keep(jnp.where(odd, across_swap_ref[...], own_swap_ref[...]), jnp.bitwise_xor(feat, 1))
    keep(pair_ref[...], jnp.bitwise_xor(feat, 2))
    keep(pair_swap_ref[...], jnp.bitwise_xor(feat, 3))
    out_ref[...] = dot_nt(full[...], block_ref[:half, :]).astype(out_ref.dtype)


def forward_own_kernel(own_ref, block_ref, total_ref):
    half = own_ref.shape[1]
    total_ref[...] = dot_nt(own_ref[...], block_ref[:half, :half])


def forward_other_kernel(total_ref, other_ref, block_ref, out_ref):
    half = other_ref.shape[1]
    total = total_ref[...] + dot_nt(other_ref[...], block_ref[:half, half:])
    out_ref[...] = total.astype(out_ref.dtype)


def backward_own_kernel(own_ref, block_ref, total_ref):
    half = own_ref.shape[1]
    total_ref[...] = dot_nn(own_ref[...], block_ref[:half, :half])


def backward_other_kernel(total_ref, other_ref, block_ref, out_ref):
    half = other_ref.shape[1]
    total = total_ref[...] + dot_nn(other_ref[...], block_ref[half:, :half])
    out_ref[...] = total.astype(out_ref.dtype)


def summed(own_ref, near_ref, across_ref):
    odd = lax.axis_index("rep") % 2 == 1
    second = jnp.where(odd, across_ref[...], own_ref[...])
    return (near_ref[...].astype(jnp.float32) + second.astype(jnp.float32)).astype(jnp.bfloat16)


def slope(value):
    part = jax.nn.sigmoid(value)
    return part * (1.0 + value * (1.0 - part))


def layer_one_kernel(own_ref, near_ref, across_ref, turned_ref, mix_ref, h_ref):
    mix = summed(own_ref, near_ref, across_ref)
    mix_ref[...] = mix
    z = dot_nn(turned_ref[...], mix)
    h_ref[...] = (z * jax.nn.sigmoid(z)).astype(h_ref.dtype)


def layer_two_kernel(
    own_ref,
    near_ref,
    turned_ref,
    weight_ref,
    cot_ref,
    cot_pair_ref,
    mix_ref,
    dz_ref,
    dm_ref,
):
    total = own_ref[...].astype(jnp.float32) + near_ref[...].astype(jnp.float32)
    mix = total.astype(jnp.bfloat16)
    mix_ref[...] = mix
    rate = slope(dot_nn(turned_ref[...], mix))
    upper = lax.axis_index("feat") // 2 == 1
    mine, pair = cot_ref[...], cot_pair_ref[...]
    quarter = mine.shape[1]
    low, high = jnp.where(upper, pair, mine), jnp.where(upper, mine, pair)
    dz_ref[:, :quarter] = (low.astype(jnp.float32) * rate[:, :quarter]).astype(jnp.bfloat16)
    dz_ref[:, quarter:] = (high.astype(jnp.float32) * rate[:, quarter:]).astype(jnp.bfloat16)
    dm_ref[...] = dot_nn(weight_ref[...], dz_ref[...]).astype(dm_ref.dtype)


def slope_kernel(mix_ref, across_ref, turned_ref, here_ref, slope_ref):
    odd = lax.axis_index("rep") % 2 == 1
    mix = jnp.where(odd, across_ref[...], mix_ref[...])
    here_ref[...] = mix
    slope_ref[...] = slope(dot_nn(turned_ref[...], mix))


def grad_kernel(mix_ref, slope_ref, out_ref):
    out_ref[...] = dot_nt(mix_ref[...], slope_ref[...])


def back_one_kernel(own_ref, near_ref, across_ref, slope_ref, dz_ref):
    dh = summed(own_ref, near_ref, across_ref)
    dz_ref[...] = (dh.astype(jnp.float32) * slope_ref[...]).astype(dz_ref.dtype)


def feature_rows(weight_ref, width):
    first = pl.multiple_of(lax.axis_index("feat") * width, width)
    return weight_ref[pl.ds(first, width), :]


def last_own_kernel(dz_ref, weight_ref, block_ref, mix_ref, total_ref, grad_ref):
    half = dz_ref.shape[1]
    own = dot_nn(feature_rows(weight_ref, total_ref.shape[0]), dz_ref[...]).astype(jnp.bfloat16)
    total_ref[...] = dot_nn(own, block_ref[:half, :])
    grad_ref[...] = dot_nt(mix_ref[...], dz_ref[...])


def message_kernel(
    total_ref,
    grad_ref,
    dz_swap_ref,
    weight_ref,
    block_ref,
    mix_swap_ref,
    two_ref,
    two_swap_ref,
    out_ref,
):
    width = total_ref.shape[0]
    hidden = weight_ref.shape[0]
    half = dz_swap_ref.shape[1]
    dz_swap = dz_swap_ref[...]
    other = dot_nn(feature_rows(weight_ref, width), dz_swap).astype(jnp.bfloat16)
    total = total_ref[...] + dot_nn(other, block_ref[half:, :])
    out_ref[:width, :] = total.astype(out_ref.dtype)
    second = lax.axis_index("feat") % 2 == 1
    grad, grad_swap = grad_ref[...], dot_nt(mix_swap_ref[...], dz_swap)
    one = jnp.where(second, grad_swap, grad) + jnp.where(second, grad, grad_swap)
    two = two_ref[...] + two_swap_ref[...]
    count = hidden // width
    for index, grad in enumerate((one, two)):
        grad = grad.astype(out_ref.dtype)
        for part in range(count):
            lane = (index * count + part) * hidden
            out_ref[width:, lane : lane + hidden] = grad[part * width : (part + 1) * width, :]


def near_kernel(own_ref, near_ref, across_ref, out_ref):
    out_ref[...] = summed(own_ref, near_ref, across_ref)


def last_kernel(scale, own_ref, far_ref, one_ref, two_ref, out_ref):
    core = lax.axis_index("feat") % 2
    width, nodes = out_ref.shape
    hidden = one_ref.shape[0]
    quarter = nodes // 4
    half = nodes // 2
    for part in range(4):
        lane = pl.multiple_of(
            jnp.bitwise_xor(part % 2, core) * half + (part // 2) * quarter, quarter
        )
        columns = pl.ds(lane, quarter)
        out_ref[:, part * quarter : (part + 1) * quarter] = (
            own_ref[:width, columns] + far_ref[:width, columns]
        )
    count = hidden // width
    for index, grad_ref in enumerate((one_ref, two_ref)):
        for part in range(count):
            lane = (index * count + part) * hidden
            total = own_ref[width:, lane : lane + hidden].astype(jnp.float32)
            total += far_ref[width:, lane : lane + hidden].astype(jnp.float32)
            grad_ref[part * width : (part + 1) * width, :] = total * scale


def paired_shards(
    features, tile_values, tile_coords, section_counts, weight_one, weight_two, cotangent
):
    hidden = weight_one.shape[0]
    width, nodes = features.shape
    side = tile_values.shape[-1]
    panels = nodes // side
    half = nodes // 2
    scale = 1.0 / math.sqrt(nodes * lax.axis_size("loop"))
    product_flops = 2 * hidden * nodes * half

    across = routed(features, to_odd_across)
    pair = routed(features, to_feature_pair)
    own_swap = routed(features, to_other_core)
    (block,) = local_call(
        functools.partial(place_kernel, panels, side),
        [bf16_array(nodes, nodes)],
        [section_counts[0, 0]]
        + [
            pltpu.with_memory_space_constraint(value, pltpu.HBM)
            for value in (tile_coords, tile_values)
        ],
        [pltpu.SMEM, pltpu.HBM, pltpu.HBM],
        [
            pltpu.SMEM((panels,), jnp.int32),
            pltpu.SMEM(tile_coords.shape, jnp.int32),
            pltpu.VMEM((panels * panels, side, side), jnp.bfloat16),
            pltpu.SemaphoreType.DMA,
            pltpu.SemaphoreType.DMA((4,)),
        ],
        flops=4_000_000_000,
    )
    one_turned, two_turned = local_call(
        turn_kernel,
        [bf16_array(hidden, hidden)] * 2,
        [weight_one, lax.optimization_barrier((weight_two, block))[0]],
    )
    across, pair, block = lax.optimization_barrier((across, pair, block))
    (part_one,) = local_call(
        first_kernel,
        [bf16_array(hidden, half)],
        [
            features,
            across,
            pair,
            own_swap,
            routed(across, to_other_core),
            routed(pair, to_other_core),
            block,
        ],
        None,
        [pltpu.VMEM((hidden, nodes), jnp.bfloat16)],
        flops=product_flops,
    )
    near_one, across_one, cot_pair = lax.optimization_barrier(
        (
            routed(part_one, to_row_owner),
            routed(part_one, to_odd_across),
            routed(lax.optimization_barrier((cotangent, part_one))[0], to_other_pair),
        )
    )
    mix_one, h_one = local_call(
        layer_one_kernel,
        [bf16_array(hidden, half)] * 2,
        [part_one, near_one, across_one, one_turned],
        None,
    )
    h_swap = routed(h_one, to_other_core)
    (total_two,) = local_call(
        forward_own_kernel, [f32_array(hidden, half)], [h_one, block], flops=product_flops // 2
    )
    (part_two,) = local_call(
        forward_other_kernel,
        [bf16_array(hidden, half)],
        [total_two, h_swap, block],
        flops=product_flops // 2,
    )
    near_two = routed(part_two, to_other_rep)
    mix_two, dz_two, dm_two = local_call(
        layer_two_kernel,
        [bf16_array(hidden, half)] * 3,
        [part_two, near_two, two_turned, weight_two, cotangent, cot_pair],
        None,
    )
    mix_across = routed(lax.optimization_barrier((mix_one, part_two))[0], to_odd_across)
    mix_here, slope_here = local_call(
        slope_kernel,
        [bf16_array(hidden, half), f32_array(hidden, half)],
        [mix_one, lax.optimization_barrier((mix_across, dm_two))[0], one_turned],
    )
    (total_three,) = local_call(
        backward_own_kernel, [f32_array(hidden, half)], [dm_two, block], flops=product_flops // 2
    )
    dm_swap, slope_here, total_three = lax.optimization_barrier(
        (routed(dm_two, to_other_core), slope_here, total_three)
    )
    (part_three,) = local_call(
        backward_other_kernel,
        [bf16_array(hidden, half)],
        [total_three, dm_swap, block],
        flops=product_flops // 2,
    )
    (grad_two,) = local_call(
        grad_kernel,
        [f32_array(hidden, hidden)],
        [lax.optimization_barrier((mix_two, part_three))[0], dz_two],
    )
    near_three, across_three, grad_two_swap, mix_swap = lax.optimization_barrier(
        (
            routed(part_three, to_column_owner),
            routed(part_three, to_odd_across),
            routed(grad_two, to_other_core),
            routed(mix_here, to_other_core),
        )
    )
    (dz_one,) = local_call(
        back_one_kernel,
        [bf16_array(hidden, half)],
        [part_three, near_three, across_three, slope_here],
    )
    dz_swap = routed(dz_one, to_other_core)
    total_four, grad_one = local_call(
        last_own_kernel,
        [f32_array(width, nodes), f32_array(hidden, hidden)],
        [dz_one, weight_one, block, mix_here],
        flops=product_flops // 2,
    )
    dz_swap, total_four = lax.optimization_barrier((dz_swap, total_four))
    (message,) = local_call(
        message_kernel,
        [bf16_array(2 * width, nodes)],
        [
            total_four,
            grad_one,
            dz_swap,
            weight_one,
            block,
            mix_swap,
            grad_two,
            grad_two_swap,
        ],
        flops=product_flops // 2,
    )
    (near_sum,) = local_call(
        near_kernel,
        [bf16_array(2 * width, nodes)],
        [message, routed(message, to_column_owner), routed(message, to_odd_across)],
    )
    return tuple(
        local_call(
            functools.partial(last_kernel, scale),
            [f32_array(hidden, hidden), f32_array(hidden, hidden), bf16_array(width, nodes)],
            [near_sum, routed(near_sum, to_far_rep, True)],
        )
    )


def solution(mesh):
    sizes = dict(mesh.shape)
    paired = sizes["loop"] == 2 and sizes["rep"] == 4 and sizes["feat"] == 4
    return jax.shard_map(
        paired_shards if paired else ring_shards,
        mesh=mesh,
        in_specs=(
            P("feat", "loop"),
            P("loop", "rep", None, None, None),
            P("loop", "rep", None, None),
            P("loop", "rep", None),
            P(),
            P(),
            P(None, ("loop", "feat")),
        ),
        out_specs=(P(), P(), P("feat", "loop")),
        check_vma=False,
    )
```

```python
import functools
import math

import jax
import jax.numpy as jnp
from jax import lax
from jax.experimental import pallas as pl
from jax.experimental.pallas import tpu as pltpu
from jax.sharding import PartitionSpec as P

tile_batch = 8


def shortened(shard):

    def short(part):
        return part.astype(jnp.bfloat16) if part.dtype == jnp.float32 else part

    return jax.tree.map(short, shard)


def passed_along(value, axis, steps):
    count = lax.axis_size(axis)
    pairs = [(source, (source + steps) % count) for source in range(count)]
    return lax.ppermute(value, axis, pairs)


def silu_slope(argument):
    sigmoid_value = jax.nn.sigmoid(argument)
    return sigmoid_value * (1.0 + argument * (1.0 - sigmoid_value))


def section_term(source, section_id, layout, transposed, enabled=True):
    tile_set, row_ids, col_ids, starts, filled, panels = layout
    feat_width = source.shape[0]
    tile_side = tile_set.shape[-1]
    slot_total = tile_set.shape[0]
    shaped = source.reshape(feat_width, panels, tile_side)
    first = starts[section_id]
    number = jnp.where(enabled, filled[section_id], 0)
    rounds = (number + tile_batch - 1) // tile_batch
    offsets = jnp.arange(tile_batch, dtype=jnp.int32)
    panel_ids = jnp.arange(panels, dtype=jnp.int32)

    def one_round(round_id, running):
        within = round_id * tile_batch + offsets
        alive_mask = within < number
        slot_ids = jnp.minimum(first + within, slot_total - 1)
        chosen = tile_set[slot_ids]
        if transposed:
            picked = shaped[:, row_ids[slot_ids], :]
            products = jnp.einsum(
                "dba,bac->dbc", picked, chosen, preferred_element_type=jnp.float32
            )
            target = col_ids[slot_ids]
        else:
            picked = shaped[:, col_ids[slot_ids], :]
            products = jnp.einsum(
                "dbc,bac->dba", picked, chosen, preferred_element_type=jnp.float32
            )
            target = row_ids[slot_ids]
        placing = ((target[:, None] == panel_ids[None, :]) & alive_mask[:, None]).astype(
            jnp.float32
        )
        return running + jnp.einsum(
            "dbe,bp->dpe", products, placing, precision=lax.Precision.HIGHEST
        )

    zero_block = jnp.zeros((feat_width, panels, tile_side), jnp.float32)
    return lax.fori_loop(0, rounds, one_round, zero_block).reshape(feat_width, panels * tile_side)


def advance(block, stride):
    return jax.tree.map(
        lambda part, own: part.astype(own.dtype),
        passed_along(shortened(block), "loop", stride),
        block,
    )


def forward_product(source, layout):
    loop_size = lax.axis_size("loop")
    rep_size = lax.axis_size("rep")
    rep_index = lax.axis_index("rep")
    sections = -(-loop_size // rep_size)
    stride = rep_size % loop_size
    current = source
    for bit in range(rep_size.bit_length() - 1):
        jump = (1 << bit) % loop_size
        if jump:
            moved = passed_along(current, "loop", jump)
            current = jnp.where((rep_index >> bit) % 2 == 1, moved, current)
    running = section_term(current, 0, layout, False)
    if sections > 1:

        def onward(step_id, carry):
            ahead, acc = carry
            ahead = advance(ahead, stride)
            return (ahead, acc + section_term(ahead, step_id, layout, False))

        ahead, running = lax.fori_loop(1, sections, onward, (current, running))
    return running


def transposed_product(source, layout):
    loop_size = lax.axis_size("loop")
    rep_size = lax.axis_size("rep")
    rep_index = lax.axis_index("rep")
    sections = -(-loop_size // rep_size)
    stride = rep_size % loop_size
    running = section_term(source, sections - 1, layout, True)
    if sections > 1:

        def backward(step_id, acc):
            acc = jax.tree.map(
                lambda part, own: part.astype(own.dtype),
                passed_along(shortened(acc), "loop", -stride),
                acc,
            )
            return acc + section_term(source, sections - 1 - step_id, layout, True)

        running = lax.fori_loop(1, sections, backward, running)
    for bit in range(rep_size.bit_length() - 1):
        jump = (1 << bit) % loop_size
        if jump:
            moved = passed_along(running.astype(jnp.bfloat16), "loop", -jump).astype(running.dtype)
            running = jnp.where((rep_index >> bit) % 2 == 1, moved, running)
    return running


def to_nodes(partial_value):
    summed = lax.psum(partial_value.astype(jnp.bfloat16), "rep")
    return lax.all_to_all(summed, "feat", split_axis=1, concat_axis=0, tiled=True)


def to_features(node_block):
    return lax.all_to_all(node_block, "feat", split_axis=0, concat_axis=1, tiled=True)


def weight_grad(mixed, slope):
    part_sum = jnp.einsum("dq,eq->de", mixed, slope, preferred_element_type=jnp.float32)
    return lax.psum(part_sum, ("loop", "feat"))


def ring_shards(features, tile_values, tile_coords, section_counts, weight_one, weight_two, cotangent):
    tile_set = tile_values[0, 0]
    row_ids = tile_coords[0, 0, 0]
    col_ids = tile_coords[0, 0, 1]
    filled = section_counts[0, 0]
    starts = jnp.cumsum(filled) - filled
    panels = features.shape[1] // tile_set.shape[-1]
    layout = (tile_set, row_ids, col_ids, starts, filled, panels)
    scale = 1.0 / math.sqrt(features.shape[1] * lax.axis_size("loop"))
    mix_one = to_nodes(forward_product(features, layout))
    z_one = jnp.einsum("de,dq->eq", weight_one, mix_one, preferred_element_type=jnp.float32)
    h_one = jax.nn.silu(z_one).astype(jnp.bfloat16)
    mix_two = to_nodes(forward_product(to_features(h_one), layout))
    z_two = jnp.einsum("de,dq->eq", weight_two, mix_two, preferred_element_type=jnp.float32)
    dz_two = (cotangent * silu_slope(z_two)).astype(jnp.bfloat16)
    grad_two = weight_grad(mix_two, dz_two) * scale
    dm_two = jnp.einsum("de,eq->dq", weight_two, dz_two, preferred_element_type=jnp.float32).astype(
        jnp.bfloat16
    )
    dh_one = to_nodes(transposed_product(to_features(dm_two), layout))
    dz_one = (dh_one * silu_slope(z_one)).astype(jnp.bfloat16)
    grad_one = weight_grad(mix_one, dz_one) * scale
    dm_one = jnp.einsum("de,eq->dq", weight_one, dz_one, preferred_element_type=jnp.float32).astype(
        jnp.bfloat16
    )
    partial_value = transposed_product(to_features(dm_one), layout)
    input_grad = lax.psum(partial_value.astype(jnp.bfloat16), "rep")
    return (grad_one, grad_two, input_grad)


mesh_axes = ("loop", "rep", "feat")
vmem_bytes = 24 * 1024 * 1024


def routed(value, target, outward=False):
    loops, reps, feats = (lax.axis_size(axis) for axis in mesh_axes)
    pairs = []
    for i in range(loops):
        for r in range(reps):
            for f in range(feats):
                idle = r >= loops
                if idle and outward:
                    continue
                to_loop, to_rep, to_feat = to_other_core(i, r, f) if idle else target(i, r, f)
                pairs.append(
                    ((i * reps + r) * feats + f, (to_loop * reps + to_rep) * feats + to_feat)
                )
    return lax.ppermute(value, mesh_axes, pairs)


def to_other_core(i, r, f):
    return i, r, f ^ 1


def to_other_pair(i, r, f):
    return i, r, f ^ 2


def to_other_loop(i, r, f):
    return 1 - i, r, f


def to_odd_across(i, r, f):
    return (1 - i, r, f) if r % 2 else (i, r, f ^ 1)


def to_other_rep(i, r, f):
    return i, r ^ 1, f


def to_row_owner(i, r, f):
    return (i, r - 1, f) if r % 2 else (1 - i, r + 1, f)


def to_column_owner(i, r, f):
    return (1 - i, r - 1, f) if r % 2 else (i, r + 1, f)


def to_far_rep(i, r, f):
    return i, r ^ 2, f


def to_far_column_owner(i, r, f):
    return (1 - i if r % 2 else i), r ^ 2, f


def to_last_column_owner(i, r, f):
    return (1 - i if r % 2 else i), r ^ 3, f


def to_feature_pair(i, r, f):
    return (1 - i if r % 2 else i), r, f ^ 2


def local_call(kernel, outs, operands, spaces=None, scratch=(), flops=0):
    spaces = spaces or [pltpu.VMEM] * len(operands)
    moved = sum(o.size * o.dtype.itemsize for o in operands) + sum(
        math.prod(o.shape) * 4 for o in outs
    )
    return pl.pallas_call(
        kernel,
        out_shape=list(outs),
        in_specs=[pl.BlockSpec(memory_space=space) for space in spaces],
        out_specs=[pl.BlockSpec(memory_space=pltpu.VMEM) for _ in outs],
        scratch_shapes=list(scratch),
        compiler_params=pltpu.CompilerParams(vmem_limit_bytes=vmem_bytes),
        cost_estimate=pl.CostEstimate(flops=flops, bytes_accessed=moved, transcendentals=0),
    )(*operands)


def bf16_array(*shape):
    return jax.ShapeDtypeStruct(shape, jnp.bfloat16)


def f32_array(*shape):
    return jax.ShapeDtypeStruct(shape, jnp.float32)


def dot_nn(a, b):
    return lax.dot_general(a, b, (((1,), (0,)), ((), ())), preferred_element_type=jnp.float32)


def dot_nt(a, b):
    return lax.dot_general(a, b, (((1,), (1,)), ((), ())), preferred_element_type=jnp.float32)


def place_kernel(
    panels,
    side,
    count_ref,
    coords_ref,
    tiles_ref,
    block_ref,
    starts,
    coords,
    held,
    list_sem,
    sems,
):
    chunks = sems.shape[0]
    size = held.shape[0] // chunks
    lists = pltpu.make_async_copy(coords_ref, coords, list_sem)
    lists.start()
    copies = []
    for chunk in range(chunks):
        here = pl.ds(chunk * size, size)
        copies.append(
            pltpu.make_async_copy(tiles_ref.at[0, 0, here], held.at[here], sems.at[chunk])
        )
        copies[-1].start()
    block_ref[...] = jnp.zeros_like(block_ref)
    quarter = panels // 4
    core = lax.axis_index("feat") % 2
    lists.wait()
    count = count_ref[0]

    for panel in range(panels):
        part, rest = divmod(panel, quarter)
        first = ((part % 2) * 2 + part // 2) * quarter + rest
        second = ((1 - part % 2) * 2 + part // 2) * quarter + rest
        starts[panel] = jnp.where(core == 0, first, second) * side

    def start_of(panel):
        return pl.multiple_of(starts[panel], side)

    def place(slot, carry):
        rows = pl.ds(start_of(coords[0, 0, 0, slot]), side)
        columns = pl.ds(start_of(coords[0, 0, 1, slot]), side)
        block_ref[rows, columns] = held[slot]
        return carry

    group = 8

    def place_group(index, carry):
        for offset in range(group):
            place(index * group + offset, carry)
        return carry

    for chunk in range(chunks):
        copies[chunk].wait()
        end = jnp.minimum(count, (chunk + 1) * size)
        whole = end // group
        lax.fori_loop(chunk * size // group, whole, place_group, 0)
        lax.fori_loop(jnp.maximum(whole * group, chunk * size), end, place, 0)


def turn_kernel(one_ref, two_ref, one_turned_ref, two_turned_ref):
    one_turned_ref[...] = one_ref[...].T
    two_turned_ref[...] = two_ref[...].T


def first_kernel(
    own_ref,
    across_ref,
    pair_ref,
    own_swap_ref,
    across_swap_ref,
    pair_swap_ref,
    block_ref,
    out_ref,
    full,
):
    width, nodes = own_ref.shape
    odd = lax.axis_index("rep") % 2 == 1
    feat = lax.axis_index("feat")
    core = feat % 2
    quarter = nodes // 4
    half = nodes // 2

    def keep(value, owner):
        row = pl.multiple_of(owner * width, width)
        for part in range(4):
            lane = pl.multiple_of(
                jnp.bitwise_xor(part % 2, core) * half + (part // 2) * quarter, quarter
            )
            full[pl.ds(row, width), pl.ds(lane, quarter)] = value[
                :, part * quarter : (part + 1) * quarter
            ]

    keep(jnp.where(odd, across_ref[...], own_ref[...]), feat)
    keep(jnp.where(odd, across_swap_ref[...], own_swap_ref[...]), jnp.bitwise_xor(feat, 1))
    keep(pair_ref[...], jnp.bitwise_xor(feat, 2))
    keep(pair_swap_ref[...], jnp.bitwise_xor(feat, 3))
    out_ref[...] = dot_nt(full[...], block_ref[:half, :]).astype(out_ref.dtype)


def forward_own_kernel(own_ref, block_ref, total_ref):
    half = own_ref.shape[1]
    total_ref[...] = dot_nt(own_ref[...], block_ref[:half, :half])


def forward_other_kernel(total_ref, other_ref, block_ref, out_ref):
    half = other_ref.shape[1]
    total = total_ref[...] + dot_nt(other_ref[...], block_ref[:half, half:])
    out_ref[...] = total.astype(out_ref.dtype)


def backward_own_kernel(own_ref, block_ref, total_ref):
    half = own_ref.shape[1]
    total_ref[...] = dot_nn(own_ref[...], block_ref[:half, :half])


def backward_other_kernel(total_ref, other_ref, block_ref, out_ref):
    half = other_ref.shape[1]
    total = total_ref[...] + dot_nn(other_ref[...], block_ref[half:, :half])
    out_ref[...] = total.astype(out_ref.dtype)


def summed(own_ref, near_ref, across_ref):
    odd = lax.axis_index("rep") % 2 == 1
    second = jnp.where(odd, across_ref[...], own_ref[...])
    return (near_ref[...].astype(jnp.float32) + second.astype(jnp.float32)).astype(jnp.bfloat16)


def slope(value):
    part = jax.nn.sigmoid(value)
    return part * (1.0 + value * (1.0 - part))


def layer_one_kernel(own_ref, near_ref, across_ref, turned_ref, mix_ref, h_ref):
    mix = summed(own_ref, near_ref, across_ref)
    mix_ref[...] = mix
    z = dot_nn(turned_ref[...], mix)
    h_ref[...] = (z * jax.nn.sigmoid(z)).astype(h_ref.dtype)


def layer_two_kernel(
    own_ref,
    near_ref,
    turned_ref,
    weight_ref,
    cot_ref,
    cot_pair_ref,
    mix_ref,
    dz_ref,
    dm_ref,
):
    total = own_ref[...].astype(jnp.float32) + near_ref[...].astype(jnp.float32)
    mix = total.astype(jnp.bfloat16)
    mix_ref[...] = mix
    rate = slope(dot_nn(turned_ref[...], mix))
    upper = lax.axis_index("feat") // 2 == 1
    mine, pair = cot_ref[...], cot_pair_ref[...]
    quarter = mine.shape[1]
    low, high = jnp.where(upper, pair, mine), jnp.where(upper, mine, pair)
    dz_ref[:, :quarter] = (low.astype(jnp.float32) * rate[:, :quarter]).astype(jnp.bfloat16)
    dz_ref[:, quarter:] = (high.astype(jnp.float32) * rate[:, quarter:]).astype(jnp.bfloat16)
    dm_ref[...] = dot_nn(weight_ref[...], dz_ref[...]).astype(dm_ref.dtype)


def slope_kernel(mix_ref, across_ref, turned_ref, here_ref, slope_ref):
    odd = lax.axis_index("rep") % 2 == 1
    mix = jnp.where(odd, across_ref[...], mix_ref[...])
    here_ref[...] = mix
    slope_ref[...] = slope(dot_nn(turned_ref[...], mix))


def grad_kernel(mix_ref, slope_ref, out_ref):
    out_ref[...] = dot_nt(mix_ref[...], slope_ref[...])


def back_one_kernel(own_ref, near_ref, across_ref, slope_ref, dz_ref):
    dh = summed(own_ref, near_ref, across_ref)
    dz_ref[...] = (dh.astype(jnp.float32) * slope_ref[...]).astype(dz_ref.dtype)


def feature_rows(weight_ref, width):
    first = pl.multiple_of(lax.axis_index("feat") * width, width)
    return weight_ref[pl.ds(first, width), :]


def last_own_kernel(dz_ref, weight_ref, block_ref, mix_ref, total_ref, grad_ref):
    half = dz_ref.shape[1]
    own = dot_nn(feature_rows(weight_ref, total_ref.shape[0]), dz_ref[...]).astype(jnp.bfloat16)
    total_ref[...] = dot_nn(own, block_ref[:half, :])
    grad_ref[...] = dot_nt(mix_ref[...], dz_ref[...])


def message_kernel(
    total_ref,
    grad_ref,
    dz_swap_ref,
    weight_ref,
    block_ref,
    mix_swap_ref,
    two_ref,
    two_swap_ref,
    out_ref,
):
    width = total_ref.shape[0]
    hidden = weight_ref.shape[0]
    half = dz_swap_ref.shape[1]
    dz_swap = dz_swap_ref[...]
    other = dot_nn(feature_rows(weight_ref, width), dz_swap).astype(jnp.bfloat16)
    total = total_ref[...] + dot_nn(other, block_ref[half:, :])
    out_ref[:width, :] = total.astype(out_ref.dtype)
    second = lax.axis_index("feat") % 2 == 1
    grad, grad_swap = grad_ref[...], dot_nt(mix_swap_ref[...], dz_swap)
    one = jnp.where(second, grad_swap, grad) + jnp.where(second, grad, grad_swap)
    two = two_ref[...] + two_swap_ref[...]
    grad = jnp.where(second, two, one).astype(out_ref.dtype)
    lines = out_ref.shape[0] - width
    for part in range(hidden // lines):
        out_ref[width:, part * hidden : (part + 1) * hidden] = grad[
            part * lines : (part + 1) * lines, :
        ]


def near_kernel(own_ref, near_ref, across_ref, out_ref):
    out_ref[...] = summed(own_ref, near_ref, across_ref)


def split_kernel(own_ref, far_ref, grad_ref):
    lines = grad_ref.shape[0]
    width = own_ref.shape[0] - lines
    grad_ref[...] = own_ref[width:, :] + far_ref[width:, :]


def total_kernel(scale, own_ref, swap_ref, one_ref, two_ref):
    second = lax.axis_index("feat") % 2 == 1
    hidden = one_ref.shape[0]
    lines = own_ref.shape[0]
    own, swap = own_ref[...], swap_ref[...]
    values = (jnp.where(second, swap, own), jnp.where(second, own, swap))
    for value, grad_ref in zip(values, (one_ref, two_ref)):
        value = value.astype(jnp.float32) * scale
        for part in range(hidden // lines):
            grad_ref[part * lines : (part + 1) * lines, :] = value[
                :, part * hidden : (part + 1) * hidden
            ]


def last_kernel(own_ref, far_ref, out_ref):
    core = lax.axis_index("feat") % 2
    width, nodes = out_ref.shape
    quarter = nodes // 4
    half = nodes // 2
    for part in range(4):
        lane = pl.multiple_of(
            jnp.bitwise_xor(part % 2, core) * half + (part // 2) * quarter, quarter
        )
        columns = pl.ds(lane, quarter)
        out_ref[:, part * quarter : (part + 1) * quarter] = (
            own_ref[:width, columns] + far_ref[:width, columns]
        )


def paired_shards(
    features, tile_values, tile_coords, section_counts, weight_one, weight_two, cotangent
):
    hidden = weight_one.shape[0]
    width, nodes = features.shape
    side = tile_values.shape[-1]
    panels = nodes // side
    half = nodes // 2
    scale = 1.0 / math.sqrt(nodes * lax.axis_size("loop"))
    product_flops = 2 * hidden * nodes * half

    across = routed(features, to_odd_across)
    pair = routed(features, to_feature_pair)
    own_swap = routed(features, to_other_core)
    (block,) = local_call(
        functools.partial(place_kernel, panels, side),
        [bf16_array(nodes, nodes)],
        [section_counts[0, 0]]
        + [
            pltpu.with_memory_space_constraint(value, pltpu.HBM)
            for value in (tile_coords, tile_values)
        ],
        [pltpu.SMEM, pltpu.HBM, pltpu.HBM],
        [
            pltpu.SMEM((panels,), jnp.int32),
            pltpu.SMEM(tile_coords.shape, jnp.int32),
            pltpu.VMEM((panels * panels, side, side), jnp.bfloat16),
            pltpu.SemaphoreType.DMA,
            pltpu.SemaphoreType.DMA((4,)),
        ],
        flops=4_000_000_000,
    )
    one_turned, two_turned = local_call(
        turn_kernel,
        [bf16_array(hidden, hidden)] * 2,
        [weight_one, lax.optimization_barrier((weight_two, block))[0]],
    )
    across, pair, block = lax.optimization_barrier((across, pair, block))
    (part_one,) = local_call(
        first_kernel,
        [bf16_array(hidden, half)],
        [
            features,
            across,
            pair,
            own_swap,
            routed(across, to_other_core),
            routed(pair, to_other_core),
            block,
        ],
        None,
        [pltpu.VMEM((hidden, nodes), jnp.bfloat16)],
        flops=product_flops,
    )
    near_one, across_one, cot_pair = lax.optimization_barrier(
        (
            routed(part_one, to_row_owner),
            routed(part_one, to_odd_across),
            routed(lax.optimization_barrier((cotangent, part_one))[0], to_other_pair),
        )
    )
    mix_one, h_one = local_call(
        layer_one_kernel,
        [bf16_array(hidden, half)] * 2,
        [part_one, near_one, across_one, one_turned],
        None,
    )
    h_swap = routed(h_one, to_other_core)
    (total_two,) = local_call(
        forward_own_kernel, [f32_array(hidden, half)], [h_one, block], flops=product_flops // 2
    )
    (part_two,) = local_call(
        forward_other_kernel,
        [bf16_array(hidden, half)],
        [total_two, h_swap, block],
        flops=product_flops // 2,
    )
    near_two = routed(part_two, to_other_rep)
    mix_two, dz_two, dm_two = local_call(
        layer_two_kernel,
        [bf16_array(hidden, half)] * 3,
        [part_two, near_two, two_turned, weight_two, cotangent, cot_pair],
        None,
    )
    mix_across = routed(lax.optimization_barrier((mix_one, part_two))[0], to_odd_across)
    mix_here, slope_here = local_call(
        slope_kernel,
        [bf16_array(hidden, half), f32_array(hidden, half)],
        [mix_one, lax.optimization_barrier((mix_across, dm_two))[0], one_turned],
    )
    (total_three,) = local_call(
        backward_own_kernel, [f32_array(hidden, half)], [dm_two, block], flops=product_flops // 2
    )
    dm_swap, slope_here, total_three = lax.optimization_barrier(
        (routed(dm_two, to_other_core), slope_here, total_three)
    )
    (part_three,) = local_call(
        backward_other_kernel,
        [bf16_array(hidden, half)],
        [total_three, dm_swap, block],
        flops=product_flops // 2,
    )
    (grad_two,) = local_call(
        grad_kernel,
        [f32_array(hidden, hidden)],
        [lax.optimization_barrier((mix_two, part_three))[0], dz_two],
    )
    near_three, across_three, grad_two_swap, mix_swap = lax.optimization_barrier(
        (
            routed(part_three, to_column_owner),
            routed(part_three, to_odd_across),
            routed(grad_two, to_other_core),
            routed(mix_here, to_other_core),
        )
    )
    (dz_one,) = local_call(
        back_one_kernel,
        [bf16_array(hidden, half)],
        [part_three, near_three, across_three, slope_here],
    )
    dz_swap = routed(dz_one, to_other_core)
    total_four, grad_one = local_call(
        last_own_kernel,
        [f32_array(width, nodes), f32_array(hidden, hidden)],
        [dz_one, weight_one, block, mix_here],
        flops=product_flops // 2,
    )
    dz_swap, total_four = lax.optimization_barrier((dz_swap, total_four))
    lines = hidden * hidden // nodes
    (message,) = local_call(
        message_kernel,
        [bf16_array(width + lines, nodes)],
        [
            total_four,
            grad_one,
            dz_swap,
            weight_one,
            block,
            mix_swap,
            grad_two,
            grad_two_swap,
        ],
        flops=product_flops // 2,
    )
    (near_sum,) = local_call(
        near_kernel,
        [bf16_array(width + lines, nodes)],
        [message, routed(message, to_column_owner), routed(message, to_odd_across)],
    )
    far_sum = routed(near_sum, to_far_rep, True)
    (grad,) = local_call(split_kernel, [bf16_array(lines, nodes)], [near_sum, far_sum])
    grad_swap = routed(grad, to_other_core)
    (input_grad,) = local_call(last_kernel, [bf16_array(width, nodes)], [near_sum, far_sum])
    grad_one, grad_two = local_call(
        functools.partial(total_kernel, scale),
        [f32_array(hidden, hidden)] * 2,
        [grad, grad_swap],
    )
    return (grad_one, grad_two, input_grad)


def solution(mesh):
    sizes = dict(mesh.shape)
    paired = sizes["loop"] == 2 and sizes["rep"] == 4 and sizes["feat"] == 4
    return jax.shard_map(
        paired_shards if paired else ring_shards,
        mesh=mesh,
        in_specs=(
            P("feat", "loop"),
            P("loop", "rep", None, None, None),
            P("loop", "rep", None, None),
            P("loop", "rep", None),
            P(),
            P(),
            P(None, ("loop", "feat")),
        ),
        out_specs=(P(), P(), P("feat", "loop")),
        check_vma=False,
    )
```

```python
import functools
import math

import jax
import jax.numpy as jnp
from jax import lax
from jax.experimental import pallas as pl
from jax.experimental.pallas import tpu as pltpu
from jax.sharding import PartitionSpec as P

tile_batch = 8


def shortened(shard):

    def short(part):
        return part.astype(jnp.bfloat16) if part.dtype == jnp.float32 else part

    return jax.tree.map(short, shard)


def passed_along(value, axis, steps):
    count = lax.axis_size(axis)
    pairs = [(source, (source + steps) % count) for source in range(count)]
    return lax.ppermute(value, axis, pairs)


def silu_slope(argument):
    sigmoid_value = jax.nn.sigmoid(argument)
    return sigmoid_value * (1.0 + argument * (1.0 - sigmoid_value))


def section_term(source, section_id, layout, transposed, enabled=True):
    tile_set, row_ids, col_ids, starts, filled, panels = layout
    feat_width = source.shape[0]
    tile_side = tile_set.shape[-1]
    slot_total = tile_set.shape[0]
    shaped = source.reshape(feat_width, panels, tile_side)
    first = starts[section_id]
    number = jnp.where(enabled, filled[section_id], 0)
    rounds = (number + tile_batch - 1) // tile_batch
    offsets = jnp.arange(tile_batch, dtype=jnp.int32)
    panel_ids = jnp.arange(panels, dtype=jnp.int32)

    def one_round(round_id, running):
        within = round_id * tile_batch + offsets
        alive_mask = within < number
        slot_ids = jnp.minimum(first + within, slot_total - 1)
        chosen = tile_set[slot_ids]
        if transposed:
            picked = shaped[:, row_ids[slot_ids], :]
            products = jnp.einsum(
                "dba,bac->dbc", picked, chosen, preferred_element_type=jnp.float32
            )
            target = col_ids[slot_ids]
        else:
            picked = shaped[:, col_ids[slot_ids], :]
            products = jnp.einsum(
                "dbc,bac->dba", picked, chosen, preferred_element_type=jnp.float32
            )
            target = row_ids[slot_ids]
        placing = ((target[:, None] == panel_ids[None, :]) & alive_mask[:, None]).astype(
            jnp.float32
        )
        return running + jnp.einsum(
            "dbe,bp->dpe", products, placing, precision=lax.Precision.HIGHEST
        )

    zero_block = jnp.zeros((feat_width, panels, tile_side), jnp.float32)
    return lax.fori_loop(0, rounds, one_round, zero_block).reshape(feat_width, panels * tile_side)


def advance(block, stride):
    return jax.tree.map(
        lambda part, own: part.astype(own.dtype),
        passed_along(shortened(block), "loop", stride),
        block,
    )


def forward_product(source, layout):
    loop_size = lax.axis_size("loop")
    rep_size = lax.axis_size("rep")
    rep_index = lax.axis_index("rep")
    sections = -(-loop_size // rep_size)
    stride = rep_size % loop_size
    current = source
    for bit in range(rep_size.bit_length() - 1):
        jump = (1 << bit) % loop_size
        if jump:
            moved = passed_along(current, "loop", jump)
            current = jnp.where((rep_index >> bit) % 2 == 1, moved, current)
    running = section_term(current, 0, layout, False)
    if sections > 1:

        def onward(step_id, carry):
            ahead, acc = carry
            ahead = advance(ahead, stride)
            return (ahead, acc + section_term(ahead, step_id, layout, False))

        ahead, running = lax.fori_loop(1, sections, onward, (current, running))
    return running


def transposed_product(source, layout):
    loop_size = lax.axis_size("loop")
    rep_size = lax.axis_size("rep")
    rep_index = lax.axis_index("rep")
    sections = -(-loop_size // rep_size)
    stride = rep_size % loop_size
    running = section_term(source, sections - 1, layout, True)
    if sections > 1:

        def backward(step_id, acc):
            acc = jax.tree.map(
                lambda part, own: part.astype(own.dtype),
                passed_along(shortened(acc), "loop", -stride),
                acc,
            )
            return acc + section_term(source, sections - 1 - step_id, layout, True)

        running = lax.fori_loop(1, sections, backward, running)
    for bit in range(rep_size.bit_length() - 1):
        jump = (1 << bit) % loop_size
        if jump:
            moved = passed_along(running.astype(jnp.bfloat16), "loop", -jump).astype(running.dtype)
            running = jnp.where((rep_index >> bit) % 2 == 1, moved, running)
    return running


def to_nodes(partial_value):
    summed = lax.psum(partial_value.astype(jnp.bfloat16), "rep")
    return lax.all_to_all(summed, "feat", split_axis=1, concat_axis=0, tiled=True)


def to_features(node_block):
    return lax.all_to_all(node_block, "feat", split_axis=0, concat_axis=1, tiled=True)


def weight_grad(mixed, slope):
    part_sum = jnp.einsum("dq,eq->de", mixed, slope, preferred_element_type=jnp.float32)
    return lax.psum(part_sum, ("loop", "feat"))


def ring_shards(features, tile_values, tile_coords, section_counts, weight_one, weight_two, cotangent):
    tile_set = tile_values[0, 0]
    row_ids = tile_coords[0, 0, 0]
    col_ids = tile_coords[0, 0, 1]
    filled = section_counts[0, 0]
    starts = jnp.cumsum(filled) - filled
    panels = features.shape[1] // tile_set.shape[-1]
    layout = (tile_set, row_ids, col_ids, starts, filled, panels)
    scale = 1.0 / math.sqrt(features.shape[1] * lax.axis_size("loop"))
    mix_one = to_nodes(forward_product(features, layout))
    z_one = jnp.einsum("de,dq->eq", weight_one, mix_one, preferred_element_type=jnp.float32)
    h_one = jax.nn.silu(z_one).astype(jnp.bfloat16)
    mix_two = to_nodes(forward_product(to_features(h_one), layout))
    z_two = jnp.einsum("de,dq->eq", weight_two, mix_two, preferred_element_type=jnp.float32)
    dz_two = (cotangent * silu_slope(z_two)).astype(jnp.bfloat16)
    grad_two = weight_grad(mix_two, dz_two) * scale
    dm_two = jnp.einsum("de,eq->dq", weight_two, dz_two, preferred_element_type=jnp.float32).astype(
        jnp.bfloat16
    )
    dh_one = to_nodes(transposed_product(to_features(dm_two), layout))
    dz_one = (dh_one * silu_slope(z_one)).astype(jnp.bfloat16)
    grad_one = weight_grad(mix_one, dz_one) * scale
    dm_one = jnp.einsum("de,eq->dq", weight_one, dz_one, preferred_element_type=jnp.float32).astype(
        jnp.bfloat16
    )
    partial_value = transposed_product(to_features(dm_one), layout)
    input_grad = lax.psum(partial_value.astype(jnp.bfloat16), "rep")
    return (grad_one, grad_two, input_grad)


mesh_axes = ("loop", "rep", "feat")
vmem_bytes = 24 * 1024 * 1024


def routed(value, target, outward=False):
    loops, reps, feats = (lax.axis_size(axis) for axis in mesh_axes)
    pairs = []
    for i in range(loops):
        for r in range(reps):
            for f in range(feats):
                idle = r >= loops
                if idle and outward:
                    continue
                to_loop, to_rep, to_feat = to_other_core(i, r, f) if idle else target(i, r, f)
                pairs.append(
                    ((i * reps + r) * feats + f, (to_loop * reps + to_rep) * feats + to_feat)
                )
    return lax.ppermute(value, mesh_axes, pairs)


def to_other_core(i, r, f):
    return i, r, f ^ 1


def to_other_pair(i, r, f):
    return i, r, f ^ 2


def to_other_loop(i, r, f):
    return 1 - i, r, f


def to_odd_across(i, r, f):
    return (1 - i, r, f) if r % 2 else (i, r, f ^ 1)


def to_other_rep(i, r, f):
    return i, r ^ 1, f


def to_row_owner(i, r, f):
    return (i, r - 1, f) if r % 2 else (1 - i, r + 1, f)


def to_column_owner(i, r, f):
    return (1 - i, r - 1, f) if r % 2 else (i, r + 1, f)


def to_far_rep(i, r, f):
    return i, r ^ 2, f


def to_far_column_owner(i, r, f):
    return (1 - i if r % 2 else i), r ^ 2, f


def to_last_column_owner(i, r, f):
    return (1 - i if r % 2 else i), r ^ 3, f


def to_feature_pair(i, r, f):
    return (1 - i if r % 2 else i), r, f ^ 2


def local_call(kernel, outs, operands, spaces=None, scratch=(), flops=0):
    spaces = spaces or [pltpu.VMEM] * len(operands)
    moved = sum(o.size * o.dtype.itemsize for o in operands) + sum(
        math.prod(o.shape) * 4 for o in outs
    )
    return pl.pallas_call(
        kernel,
        out_shape=list(outs),
        in_specs=[pl.BlockSpec(memory_space=space) for space in spaces],
        out_specs=[pl.BlockSpec(memory_space=pltpu.VMEM) for _ in outs],
        scratch_shapes=list(scratch),
        compiler_params=pltpu.CompilerParams(vmem_limit_bytes=vmem_bytes),
        cost_estimate=pl.CostEstimate(flops=flops, bytes_accessed=moved, transcendentals=0),
    )(*operands)


def bf16_array(*shape):
    return jax.ShapeDtypeStruct(shape, jnp.bfloat16)


def f32_array(*shape):
    return jax.ShapeDtypeStruct(shape, jnp.float32)


def dot_nn(a, b):
    return lax.dot_general(a, b, (((1,), (0,)), ((), ())), preferred_element_type=jnp.float32)


def dot_nt(a, b):
    return lax.dot_general(a, b, (((1,), (1,)), ((), ())), preferred_element_type=jnp.float32)


def place_kernel(
    panels,
    side,
    count_ref,
    coords_ref,
    tiles_ref,
    block_ref,
    turned_ref,
    starts,
    coords,
    held,
    list_sem,
    sems,
):
    chunks = sems.shape[0]
    size = held.shape[0] // chunks
    lists = pltpu.make_async_copy(coords_ref, coords, list_sem)
    lists.start()
    copies = []
    for chunk in range(chunks):
        here = pl.ds(chunk * size, size)
        copies.append(
            pltpu.make_async_copy(tiles_ref.at[0, 0, here], held.at[here], sems.at[chunk])
        )
        copies[-1].start()
    block_ref[...] = jnp.zeros_like(block_ref)
    turned_ref[...] = jnp.zeros_like(turned_ref)
    half = turned_ref.shape[1]
    quarter = panels // 4
    core = lax.axis_index("feat") % 2
    lists.wait()
    count = count_ref[0]

    for panel in range(panels):
        part, rest = divmod(panel, quarter)
        first = ((part % 2) * 2 + part // 2) * quarter + rest
        second = ((1 - part % 2) * 2 + part // 2) * quarter + rest
        starts[panel] = jnp.where(core == 0, first, second) * side

    def start_of(panel):
        return pl.multiple_of(starts[panel], side)

    def place(slot, carry):
        row = start_of(coords[0, 0, 0, slot])
        columns = pl.ds(start_of(coords[0, 0, 1, slot]), side)
        block_ref[pl.ds(row, side), columns] = held[slot]

        @pl.when(row < half)
        def _():
            turned_ref[columns, pl.ds(row, side)] = held[slot].T

        return carry

    group = 8

    def place_group(index, carry):
        for offset in range(group):
            place(index * group + offset, carry)
        return carry

    for chunk in range(chunks):
        copies[chunk].wait()
        end = jnp.minimum(count, (chunk + 1) * size)
        whole = end // group
        lax.fori_loop(chunk * size // group, whole, place_group, 0)
        lax.fori_loop(jnp.maximum(whole * group, chunk * size), end, place, 0)


def turn_kernel(one_ref, two_ref, one_turned_ref, two_turned_ref):
    one_turned_ref[...] = one_ref[...].T
    two_turned_ref[...] = two_ref[...].T


def first_kernel(
    own_ref,
    across_ref,
    pair_ref,
    own_swap_ref,
    across_swap_ref,
    pair_swap_ref,
    block_ref,
    out_ref,
    full,
):
    width, nodes = own_ref.shape
    odd = lax.axis_index("rep") % 2 == 1
    feat = lax.axis_index("feat")
    core = feat % 2
    quarter = nodes // 4
    half = nodes // 2

    def keep(value, owner):
        row = pl.multiple_of(owner * width, width)
        for part in range(4):
            lane = pl.multiple_of(
                jnp.bitwise_xor(part % 2, core) * half + (part // 2) * quarter, quarter
            )
            full[pl.ds(row, width), pl.ds(lane, quarter)] = value[
                :, part * quarter : (part + 1) * quarter
            ]

    keep(jnp.where(odd, across_ref[...], own_ref[...]), feat)
    keep(jnp.where(odd, across_swap_ref[...], own_swap_ref[...]), jnp.bitwise_xor(feat, 1))
    keep(pair_ref[...], jnp.bitwise_xor(feat, 2))
    keep(pair_swap_ref[...], jnp.bitwise_xor(feat, 3))
    out_ref[...] = dot_nn(full[...], block_ref[...]).astype(out_ref.dtype)


def forward_own_kernel(own_ref, block_ref, total_ref):
    half = own_ref.shape[1]
    total_ref[...] = dot_nn(own_ref[...], block_ref[:half, :])


def forward_other_kernel(total_ref, other_ref, block_ref, out_ref):
    half = other_ref.shape[1]
    total = total_ref[...] + dot_nn(other_ref[...], block_ref[half:, :])
    out_ref[...] = total.astype(out_ref.dtype)


def backward_own_kernel(own_ref, block_ref, total_ref):
    half = own_ref.shape[1]
    total_ref[...] = dot_nn(own_ref[...], block_ref[:half, :half])


def backward_other_kernel(total_ref, other_ref, block_ref, out_ref):
    half = other_ref.shape[1]
    total = total_ref[...] + dot_nn(other_ref[...], block_ref[half:, :half])
    out_ref[...] = total.astype(out_ref.dtype)


def summed(own_ref, near_ref, across_ref):
    odd = lax.axis_index("rep") % 2 == 1
    second = jnp.where(odd, across_ref[...], own_ref[...])
    return (near_ref[...].astype(jnp.float32) + second.astype(jnp.float32)).astype(jnp.bfloat16)


def slope(value):
    part = jax.nn.sigmoid(value)
    return part * (1.0 + value * (1.0 - part))


def layer_one_kernel(own_ref, near_ref, across_ref, turned_ref, mix_ref, h_ref):
    mix = summed(own_ref, near_ref, across_ref)
    mix_ref[...] = mix
    z = dot_nn(turned_ref[...], mix)
    h_ref[...] = (z * jax.nn.sigmoid(z)).astype(h_ref.dtype)


def layer_two_kernel(
    own_ref,
    near_ref,
    turned_ref,
    weight_ref,
    cot_ref,
    cot_pair_ref,
    mix_ref,
    dz_ref,
    dm_ref,
):
    total = own_ref[...].astype(jnp.float32) + near_ref[...].astype(jnp.float32)
    mix = total.astype(jnp.bfloat16)
    mix_ref[...] = mix
    rate = slope(dot_nn(turned_ref[...], mix))
    upper = lax.axis_index("feat") // 2 == 1
    mine, pair = cot_ref[...], cot_pair_ref[...]
    quarter = mine.shape[1]
    low, high = jnp.where(upper, pair, mine), jnp.where(upper, mine, pair)
    dz_ref[:, :quarter] = (low.astype(jnp.float32) * rate[:, :quarter]).astype(jnp.bfloat16)
    dz_ref[:, quarter:] = (high.astype(jnp.float32) * rate[:, quarter:]).astype(jnp.bfloat16)
    dm_ref[...] = dot_nn(weight_ref[...], dz_ref[...]).astype(dm_ref.dtype)


def slope_kernel(mix_ref, across_ref, turned_ref, here_ref, slope_ref):
    odd = lax.axis_index("rep") % 2 == 1
    mix = jnp.where(odd, across_ref[...], mix_ref[...])
    here_ref[...] = mix
    slope_ref[...] = slope(dot_nn(turned_ref[...], mix))


def grad_kernel(mix_ref, slope_ref, out_ref):
    out_ref[...] = dot_nt(mix_ref[...], slope_ref[...])


def back_one_kernel(own_ref, near_ref, across_ref, slope_ref, dz_ref):
    dh = summed(own_ref, near_ref, across_ref)
    dz_ref[...] = (dh.astype(jnp.float32) * slope_ref[...]).astype(dz_ref.dtype)


def feature_rows(weight_ref, width):
    first = pl.multiple_of(lax.axis_index("feat") * width, width)
    return weight_ref[pl.ds(first, width), :]


def last_own_kernel(dz_ref, weight_ref, block_ref, mix_ref, total_ref, grad_ref):
    half = dz_ref.shape[1]
    own = dot_nn(feature_rows(weight_ref, total_ref.shape[0]), dz_ref[...]).astype(jnp.bfloat16)
    total_ref[...] = dot_nn(own, block_ref[:half, :])
    grad_ref[...] = dot_nt(mix_ref[...], dz_ref[...])


def message_kernel(
    total_ref,
    grad_ref,
    dz_swap_ref,
    weight_ref,
    block_ref,
    mix_swap_ref,
    two_ref,
    two_swap_ref,
    out_ref,
):
    width = total_ref.shape[0]
    hidden = weight_ref.shape[0]
    half = dz_swap_ref.shape[1]
    dz_swap = dz_swap_ref[...]
    other = dot_nn(feature_rows(weight_ref, width), dz_swap).astype(jnp.bfloat16)
    total = total_ref[...] + dot_nn(other, block_ref[half:, :])
    out_ref[:width, :] = total.astype(out_ref.dtype)
    second = lax.axis_index("feat") % 2 == 1
    grad, grad_swap = grad_ref[...], dot_nt(mix_swap_ref[...], dz_swap)
    one = jnp.where(second, grad_swap, grad) + jnp.where(second, grad, grad_swap)
    two = two_ref[...] + two_swap_ref[...]
    grad = jnp.where(second, two, one).astype(out_ref.dtype)
    lines = out_ref.shape[0] - width
    for part in range(hidden // lines):
        out_ref[width:, part * hidden : (part + 1) * hidden] = grad[
            part * lines : (part + 1) * lines, :
        ]


def near_kernel(own_ref, near_ref, across_ref, out_ref):
    out_ref[...] = summed(own_ref, near_ref, across_ref)


def split_kernel(own_ref, far_ref, grad_ref):
    lines = grad_ref.shape[0]
    width = own_ref.shape[0] - lines
    grad_ref[...] = own_ref[width:, :] + far_ref[width:, :]


def total_kernel(scale, own_ref, swap_ref, one_ref, two_ref):
    second = lax.axis_index("feat") % 2 == 1
    hidden = one_ref.shape[0]
    lines = own_ref.shape[0]
    own, swap = own_ref[...], swap_ref[...]
    values = (jnp.where(second, swap, own), jnp.where(second, own, swap))
    for value, grad_ref in zip(values, (one_ref, two_ref)):
        value = value.astype(jnp.float32) * scale
        for part in range(hidden // lines):
            grad_ref[part * lines : (part + 1) * lines, :] = value[
                :, part * hidden : (part + 1) * hidden
            ]


def last_kernel(own_ref, far_ref, out_ref):
    core = lax.axis_index("feat") % 2
    width, nodes = out_ref.shape
    quarter = nodes // 4
    half = nodes // 2
    for part in range(4):
        lane = pl.multiple_of(
            jnp.bitwise_xor(part % 2, core) * half + (part // 2) * quarter, quarter
        )
        columns = pl.ds(lane, quarter)
        out_ref[:, part * quarter : (part + 1) * quarter] = (
            own_ref[:width, columns] + far_ref[:width, columns]
        )


def paired_shards(
    features, tile_values, tile_coords, section_counts, weight_one, weight_two, cotangent
):
    hidden = weight_one.shape[0]
    width, nodes = features.shape
    side = tile_values.shape[-1]
    panels = nodes // side
    half = nodes // 2
    scale = 1.0 / math.sqrt(nodes * lax.axis_size("loop"))
    product_flops = 2 * hidden * nodes * half

    across = routed(features, to_odd_across)
    pair = routed(features, to_feature_pair)
    own_swap = routed(features, to_other_core)
    block, turned = local_call(
        functools.partial(place_kernel, panels, side),
        [bf16_array(nodes, nodes), bf16_array(nodes, half)],
        [section_counts[0, 0]]
        + [
            pltpu.with_memory_space_constraint(value, pltpu.HBM)
            for value in (tile_coords, tile_values)
        ],
        [pltpu.SMEM, pltpu.HBM, pltpu.HBM],
        [
            pltpu.SMEM((panels,), jnp.int32),
            pltpu.SMEM(tile_coords.shape, jnp.int32),
            pltpu.VMEM((panels * panels, side, side), jnp.bfloat16),
            pltpu.SemaphoreType.DMA,
            pltpu.SemaphoreType.DMA((4,)),
        ],
        flops=4_000_000_000,
    )
    one_turned, two_turned = local_call(
        turn_kernel,
        [bf16_array(hidden, hidden)] * 2,
        [weight_one, lax.optimization_barrier((weight_two, block))[0]],
    )
    across, pair, block, turned = lax.optimization_barrier((across, pair, block, turned))
    (part_one,) = local_call(
        first_kernel,
        [bf16_array(hidden, half)],
        [
            features,
            across,
            pair,
            own_swap,
            routed(across, to_other_core),
            routed(pair, to_other_core),
            turned,
        ],
        None,
        [pltpu.VMEM((hidden, nodes), jnp.bfloat16)],
        flops=product_flops,
    )
    near_one, across_one, cot_pair = lax.optimization_barrier(
        (
            routed(part_one, to_row_owner),
            routed(part_one, to_odd_across),
            routed(lax.optimization_barrier((cotangent, part_one))[0], to_other_pair),
        )
    )
    mix_one, h_one = local_call(
        layer_one_kernel,
        [bf16_array(hidden, half)] * 2,
        [part_one, near_one, across_one, one_turned],
        None,
    )
    h_swap = routed(h_one, to_other_core)
    (total_two,) = local_call(
        forward_own_kernel, [f32_array(hidden, half)], [h_one, turned], flops=product_flops // 2
    )
    (part_two,) = local_call(
        forward_other_kernel,
        [bf16_array(hidden, half)],
        [total_two, h_swap, turned],
        flops=product_flops // 2,
    )
    near_two = routed(part_two, to_other_rep)
    mix_two, dz_two, dm_two = local_call(
        layer_two_kernel,
        [bf16_array(hidden, half)] * 3,
        [part_two, near_two, two_turned, weight_two, cotangent, cot_pair],
        None,
    )
    mix_across = routed(lax.optimization_barrier((mix_one, part_two))[0], to_odd_across)
    mix_here, slope_here = local_call(
        slope_kernel,
        [bf16_array(hidden, half), f32_array(hidden, half)],
        [mix_one, lax.optimization_barrier((mix_across, dm_two))[0], one_turned],
    )
    (total_three,) = local_call(
        backward_own_kernel, [f32_array(hidden, half)], [dm_two, block], flops=product_flops // 2
    )
    dm_swap, slope_here, total_three = lax.optimization_barrier(
        (routed(dm_two, to_other_core), slope_here, total_three)
    )
    (part_three,) = local_call(
        backward_other_kernel,
        [bf16_array(hidden, half)],
        [total_three, dm_swap, block],
        flops=product_flops // 2,
    )
    (grad_two,) = local_call(
        grad_kernel,
        [f32_array(hidden, hidden)],
        [lax.optimization_barrier((mix_two, part_three))[0], dz_two],
    )
    near_three, across_three, grad_two_swap, mix_swap = lax.optimization_barrier(
        (
            routed(part_three, to_column_owner),
            routed(part_three, to_odd_across),
            routed(grad_two, to_other_core),
            routed(mix_here, to_other_core),
        )
    )
    (dz_one,) = local_call(
        back_one_kernel,
        [bf16_array(hidden, half)],
        [part_three, near_three, across_three, slope_here],
    )
    dz_swap = routed(dz_one, to_other_core)
    total_four, grad_one = local_call(
        last_own_kernel,
        [f32_array(width, nodes), f32_array(hidden, hidden)],
        [dz_one, weight_one, block, mix_here],
        flops=product_flops // 2,
    )
    dz_swap, total_four = lax.optimization_barrier((dz_swap, total_four))
    lines = hidden * hidden // nodes
    (message,) = local_call(
        message_kernel,
        [bf16_array(width + lines, nodes)],
        [
            total_four,
            grad_one,
            dz_swap,
            weight_one,
            block,
            mix_swap,
            grad_two,
            grad_two_swap,
        ],
        flops=product_flops // 2,
    )
    (near_sum,) = local_call(
        near_kernel,
        [bf16_array(width + lines, nodes)],
        [message, routed(message, to_column_owner), routed(message, to_odd_across)],
    )
    far_sum = routed(near_sum, to_far_rep, True)
    (grad,) = local_call(split_kernel, [bf16_array(lines, nodes)], [near_sum, far_sum])
    grad_swap = routed(grad, to_other_core)
    (input_grad,) = local_call(last_kernel, [bf16_array(width, nodes)], [near_sum, far_sum])
    grad_one, grad_two = local_call(
        functools.partial(total_kernel, scale),
        [f32_array(hidden, hidden)] * 2,
        [grad, grad_swap],
    )
    return (grad_one, grad_two, input_grad)


def solution(mesh):
    sizes = dict(mesh.shape)
    paired = sizes["loop"] == 2 and sizes["rep"] == 4 and sizes["feat"] == 4
    return jax.shard_map(
        paired_shards if paired else ring_shards,
        mesh=mesh,
        in_specs=(
            P("feat", "loop"),
            P("loop", "rep", None, None, None),
            P("loop", "rep", None, None),
            P("loop", "rep", None),
            P(),
            P(),
            P(None, ("loop", "feat")),
        ),
        out_specs=(P(), P(), P("feat", "loop")),
        check_vma=False,
    )
```
